512 devices in a mesh: seq: 32 (over y, z_lo), ch: 16 (over x, z_hi, core).
Axes of the slice: x: 4, y: 4, z: 16 (z_hi: 2, z_lo: 8; z = z_hi * 8 + z_lo), core: 2. Of those that a mesh axis runs over, the one named last changes fastest.
Arguments:
- query_act: bfloat16 [8192, 8192], P('seq', 'ch'), may hold values from -6 to 6
- key_act: bfloat16 [8192, 8192], P('seq', 'ch'), may hold values from -6 to 6
- value_act: bfloat16 [8192, 8192], P('seq', 'ch'), may hold values from -110 to 110
- conv_out: bfloat16 [8192, 8192], P('seq', 'ch'), may hold values from -110 to 110
- grad_out: bfloat16 [8192, 8192], P('seq', 'ch'), may hold values from -6 to 6
- norm_gain: float32 [16, 512], P('ch'), may hold values from 0.5 to 1.5
- skip_gain: float32 [16, 512], P('ch', 'seq'), may hold values from 0.25 to 2
- filters: float32 [16, 512, 8192], P('ch', 'seq'), may hold values from -6 to 6
- row_prev: float32 [16, 8192], P('ch', 'seq'), may hold values from 0.1 to 2
- col_prev: float32 [16, 512], P('ch', 'seq'), may hold values from 0.1 to 2
Outputs:
- grad_query: bfloat16 [8192, 8192], P('seq', 'ch')
- grad_key: bfloat16 [8192, 8192], P('seq', 'ch')
- grad_value: bfloat16 [8192, 8192], P('seq', 'ch')
- grad_filters: float32 [16, 512, 8192], P('ch', 'seq')
- grad_gain: float32 [16, 512], P('ch', 'seq')
- grad_skip: float32 [16, 512], P('ch', 'seq')
- row_moment: float32 [16, 8192], P('ch', 'seq')
- col_moment: float32 [16, 512], P('ch', 'seq')
The draws below stay inside these ranges and needn't reach their ends.
All inputs are finite; a program needn't handle non-finite values.
Results may differ from the reference program's by a relative error of at most 0.013.
Values may be sent and summed in bfloat16 or wider, within the bound.
No kernel may reach another device: no remote copies, remote signals or barrier semaphores. Data moves between devices by JAX's collectives and lax.ppermute only.
A program may use at most 64 MiB of HBM per device.

```python
import math
import jax
import jax.numpy as jnp
from jax import lax

D = 8192
SEQ_LEN = 8192
N_CH = 16


def field_scales(key, row_lo, row_hi):
    first_key, second_key = jax.random.split(key)
    row_scales = jnp.exp(jax.random.uniform(first_key, (SEQ_LEN, 1), jnp.float32, math.log(row_lo), math.log(row_hi)))
    col_scales = jnp.exp(jax.random.uniform(second_key, (1, D), jnp.float32, math.log(0.3), math.log(3.0)))
    rising = jnp.exp(math.log(3.0) * jnp.arange(D, dtype=jnp.float32)[None, :] / D)
    return row_scales * col_scales * rising


def draw_conv_out(key, part):
    key = jax.random.fold_in(key, 11)
    scale_key, base_key = jax.random.split(key, 2)
    scales = field_scales(scale_key, 0.3, 3.0)
    base_field = jnp.clip(jax.random.normal(base_key, (SEQ_LEN, D), jnp.float32), -4.0, 4.0)
    return (base_field * scales).astype(jnp.bfloat16)


def draw_value_act(key, part):
    key = jax.random.fold_in(key, 12)
    scale_key, base_key = jax.random.split(key, 2)
    scales = field_scales(scale_key, 0.5, 2.0)
    base_field = jnp.clip(jax.random.normal(base_key, (SEQ_LEN, D), jnp.float32), -4.0, 4.0)
    return (base_field * scales).astype(jnp.bfloat16)


def levels(key, dims, pieces, least, largest):
    def one(axis_at, blocks):
        steps = jax.random.uniform(jax.random.fold_in(jax.random.fold_in(key, 6), axis_at), (blocks,), jnp.float32, least / len(pieces), largest / len(pieces))
        return jnp.repeat(jnp.exp(steps), dims[axis_at] // blocks).reshape((-1,) + (1,) * (len(dims) - axis_at - 1))

    factor_of = one(*pieces[0])
    for cut in pieces[1:]:
        factor_of = factor_of * one(*cut)
    return factor_of


def noise(stream_key, dims, deviation, limit, cuts=(), kind=jnp.bfloat16):
    loudness = levels(stream_key, dims, cuts, -0.22, 0.18) if cuts else 1.0
    array = jax.random.normal(stream_key, dims, jnp.float32) * deviation * loudness
    return jnp.minimum(jnp.maximum(array, -limit), limit).astype(kind)


def setup_inputs(seed: int = 0) -> dict:
    keys = jax.random.split(jax.random.key(seed), 11)
    return {
        "query_act": noise(keys[0], (SEQ_LEN, D), 1.0, 6.0, ((0, 32), (1, 16))),
        "key_act": noise(keys[1], (SEQ_LEN, D), 1.0, 6.0, ((0, 32), (1, 16))),
        "value_act": draw_value_act(jax.random.fold_in(keys[10], 71), 0),
        "conv_out": draw_conv_out(jax.random.fold_in(keys[10], 71), 0),
        "grad_out": noise(keys[4], (SEQ_LEN, D), 1.0, 6.0, ((0, 32), (1, 16))),
        "norm_gain": jnp.clip(0.5 + 1.0 * jax.random.uniform(keys[5], (N_CH, D // N_CH), jnp.float32) ** levels(keys[5], (N_CH, D // N_CH), ((0, 16),), -0.2, 0.2), 0.5, 1.5),
        "skip_gain": jnp.clip(0.25 + 1.75 * jax.random.uniform(keys[6], (N_CH, D // N_CH), jnp.float32) ** levels(keys[6], (N_CH, D // N_CH), ((0, 16), (1, 32)), -0.2, 0.2), 0.25, 2.0),
        "filters": noise(keys[7], (N_CH, D // N_CH, SEQ_LEN), 1.0, 6.0, ((0, 16), (1, 32)), jnp.float32),
        "row_prev": jnp.clip(jnp.exp(math.log(2.0) - 2.9957323 * jax.random.uniform(keys[8], (N_CH, SEQ_LEN), jnp.float32) ** levels(keys[8], (N_CH, SEQ_LEN), ((0, 16), (1, 32)), -0.2, 0.2)), 0.1, 2.0),
        "col_prev": jnp.clip(jnp.exp(math.log(2.0) - 2.9957323 * jax.random.uniform(keys[9], (N_CH, D // N_CH), jnp.float32) ** levels(keys[9], (N_CH, D // N_CH), ((0, 16), (1, 32)), -0.2, 0.2)), 0.1, 2.0),
    }


EPS_NORM = 1e-05
EPS_MOMENT = 1e-30
DECAY = 1.0 - 2.0 ** (-0.8)

def correlate(first, second, seq_span):
    padded = 2 * seq_span
    first_spec = jnp.fft.rfft(first, n=padded, axis=1)
    second_spec = jnp.fft.rfft(second, n=padded, axis=1)
    return jnp.fft.irfft(first_spec * jnp.conj(second_spec), n=padded, axis=1)[:, :seq_span]

def reference(query_act, key_act, value_act, conv_out, grad_out, norm_gain, skip_gain, filters, row_prev, col_prev):
    query32 = query_act.astype(jnp.float32)
    key32 = key_act.astype(jnp.float32)
    value32 = value_act.astype(jnp.float32)
    conv32 = conv_out.astype(jnp.float32)
    gain_row = norm_gain.reshape(1, D)
    gated_out = query32 * conv32
    inv_rms = lax.rsqrt(lax.optimization_barrier(jnp.mean(gated_out * gated_out, axis=1, keepdims=True)) + EPS_NORM)
    cotangent = grad_out.astype(jnp.float32)
    scaled = cotangent * gain_row
    grad_gain = lax.optimization_barrier(jnp.sum(cotangent * gated_out * inv_rms, axis=0)).reshape(N_CH, D // N_CH)
    mean_dot = lax.optimization_barrier(jnp.mean(scaled * gated_out, axis=1, keepdims=True))
    grad_gated = inv_rms * (scaled - gated_out * inv_rms * inv_rms * mean_dot)
    grad_query = (grad_gated * conv32).astype(jnp.bfloat16)
    grad_conv = (grad_gated * query32).astype(jnp.bfloat16)
    mixed_act = (key32 * value32).astype(jnp.bfloat16)
    filt_scale = 1.0 / math.sqrt(SEQ_LEN)
    block_size = min(D, 512)
    groups = D // block_size
    conv_cols = grad_conv.astype(jnp.float32).T.reshape(groups, block_size, SEQ_LEN)
    mixed_cols = mixed_act.astype(jnp.float32).T.reshape(groups, block_size, SEQ_LEN)
    filt_cols = filters.reshape(groups, block_size, SEQ_LEN) * filt_scale
    skip_cols = skip_gain.reshape(groups, block_size, 1)

    def per_group(operands):
        conv_part, mixed_part, filt_part, skip_part = operands
        grad_part = correlate(conv_part, filt_part, SEQ_LEN) + skip_part * conv_part
        filt_grad = correlate(conv_part, mixed_part, SEQ_LEN) * filt_scale
        skip_grad = lax.optimization_barrier(jnp.sum(conv_part * mixed_part, axis=1))
        return (grad_part, filt_grad, skip_grad)
    grad_mix, grad_filt, grad_skip = lax.map(per_group, (conv_cols, mixed_cols, filt_cols, skip_cols))
    grad_mix = grad_mix.reshape(D, SEQ_LEN).T
    grad_key = (grad_mix * value32).astype(jnp.bfloat16)
    grad_value = (grad_mix * key32).astype(jnp.bfloat16)
    grad_filt = grad_filt.reshape(D, SEQ_LEN)
    squares = grad_filt * grad_filt + EPS_MOMENT
    group_rows = lax.optimization_barrier(jnp.mean(squares.reshape(N_CH, D // N_CH, SEQ_LEN), axis=1))
    row_moment = DECAY * row_prev + (1.0 - DECAY) * group_rows
    col_moment = DECAY * col_prev + (1.0 - DECAY) * lax.optimization_barrier(jnp.mean(squares, axis=1)).reshape(N_CH, D // N_CH)
    return (grad_query, grad_key, grad_value, grad_filt.reshape(N_CH, D // N_CH, SEQ_LEN), grad_gain, grad_skip.reshape(N_CH, D // N_CH), row_moment, col_moment)
```

```python
import functools
import math

import jax
import jax.numpy as jnp
from jax import lax
from jax.experimental import pallas as pl
from jax.experimental.pallas import tpu as pltpu
from jax.sharding import PartitionSpec as P

EPS_NORM = 1e-05
EPS_MOMENT = 1e-30
DECAY = 1.0 - 2.0 ** (-0.8)
F32 = jnp.float32
BF16 = jnp.bfloat16
LANE = 128
VMEM_LIMIT = 48 << 20


def iota(shape, axis):
    return lax.broadcasted_iota(jnp.int32, shape, axis)


def reversal():
    return jnp.where(iota((LANE, LANE), 0) + iota((LANE, LANE), 1) == LANE - 1, 1.0, 0.0).astype(BF16)


def kernel_call(body, outs, args, scratch=(), flops=0):
    total = sum(math.prod(a.shape) * a.dtype.itemsize for a in list(args) + list(outs))
    return pl.pallas_call(
        body,
        out_shape=tuple(outs),
        in_specs=[pl.BlockSpec(memory_space=pltpu.VMEM)] * len(args),
        out_specs=tuple(pl.BlockSpec(memory_space=pltpu.VMEM) for _ in outs),
        scratch_shapes=list(scratch),
        compiler_params=pltpu.CompilerParams(vmem_limit_bytes=VMEM_LIMIT),
        cost_estimate=pl.CostEstimate(flops=flops, bytes_accessed=total, transcendentals=0),
    )(*args)


def shape(dims, dtype):
    return jax.ShapeDtypeStruct(dims, dtype)


def token_sums(query, conv, cot, gain, out):
    gated = query[...].astype(F32) * conv[...].astype(F32)
    scaled = cot[...].astype(F32) * gain[...]
    width = gated.shape[1]

    def fold(x):
        part = sum(x[:, k : k + LANE] for k in range(0, width, LANE))
        cols = [
            jnp.sum(part[r : r + LANE].T, axis=0, keepdims=True) for r in range(0, part.shape[0], LANE)
        ]
        return jnp.concatenate(cols, axis=1)

    both = jnp.concatenate([fold(gated * gated), fold(scaled * gated)], axis=0)
    for peer in range(out.shape[0]):
        out[peer] = both


def mix_columns(key, value, out):
    mixed = (key[...].astype(F32) * value[...].astype(F32)).astype(BF16).astype(F32)
    flip = reversal()
    for cb in range(mixed.shape[1] // LANE):
        for half in range(mixed.shape[0] // LANE):
            block = mixed[half * LANE : (half + 1) * LANE, cb * LANE : (cb + 1) * LANE].T.astype(BF16)
            block = jnp.dot(block, flip, preferred_element_type=F32).astype(BF16)
            for d in range(8):
                out[cb * 8 + d, half * 16 : half * 16 + 16, :] = block[d * 16 : d * 16 + 16, :]


def filter_rows(filt, out):
    flip = reversal()
    for b in range(filt.shape[1] // LANE):
        block = filt[:, b * LANE : (b + 1) * LANE].astype(BF16)
        out[b * 16 : b * 16 + 16, :] = jnp.dot(block, flip, preferred_element_type=F32).astype(BF16)


def token_grads(total_width, query, conv, cot, gain, sums, grad_query, conv_cols, gain_part):
    totals = jnp.sum(sums[...], axis=0)
    inv_row = lax.rsqrt(totals[0:1, :] / total_width + EPS_NORM)
    back_row = inv_row * inv_row * (totals[1:2, :] / total_width)
    rows = query.shape[0]
    both = jnp.concatenate([inv_row, back_row, jnp.zeros((6, rows), F32)], axis=0)
    for half in range(rows // LANE):
        lo = half * LANE
        cols = jnp.concatenate([both[:, lo : lo + LANE]] * (LANE // 8), axis=0).T
        inv = cols[:, 0:1]
        back = cols[:, 1:2]
        for cb in range(query.shape[1] // LANE):
            at = (slice(lo, lo + LANE), slice(cb * LANE, (cb + 1) * LANE))
            query32 = query[at].astype(F32)
            conv32 = conv[at].astype(F32)
            cot32 = cot[at].astype(F32)
            gated = query32 * conv32
            grad = inv * (cot32 * gain[:, at[1]] - gated * back)
            grad_query[at] = (grad * conv32).astype(BF16)
            block = (grad * query32).T.astype(BF16)
            for d in range(8):
                conv_cols[cb * 8 + d, half * 16 : half * 16 + 16, :] = block[d * 16 : d * 16 + 16, :]
            part = jnp.sum(cot32 * gated * inv, axis=0, keepdims=True)
            if half == 0:
                gain_part[:, at[1]] = part
            else:
                gain_part[:, at[1]] += part


def correlations(
    n_blocks, scale, group, conv_cols, mixed_cols, filt, skip, gain_part, col_prev,
    back, grad_filt, grad_skip, col_moment,
    conv_s, mix_s, filt_s, hankel, conv_c, cols_c, mix_out, filt_out,
):
    chans = 16
    peers = n_blocks // 2
    row, lane = iota((LANE, LANE), 0), iota((LANE, LANE), 1)
    keep = lane <= row
    for d in range(peers):
        at = slice(d * 32, d * 32 + 32)
        conv_s[at, :] = conv_cols[d].astype(F32)
        mix_s[at, :] = mixed_cols[d].astype(F32)
        filt_s[at, :] = filt[at, :].astype(F32)
    for b in range(2):
        conv_c[b, n_blocks : n_blocks + 8, :] = jnp.zeros((8, LANE), F32)
        for i in range(2):
            cols_c[b, i, 0:n_blocks, :] = jnp.zeros((n_blocks, LANE), F32)

    def build(c, b):
        conv_c[b, 0:n_blocks, :] = conv_s[pl.ds(c, n_blocks, stride=chans), :]
        cols_c[b, 0, n_blocks:, :] = filt_s[pl.ds(c, n_blocks, stride=chans), :]
        cols_c[b, 1, n_blocks:, :] = mix_s[pl.ds(c, n_blocks, stride=chans), :]

        def turned(k):
            wide = jnp.broadcast_to(conv_c[b, k : k + 1, :], (LANE, LANE))
            return pltpu.roll(wide, 1, axis=1, stride=1, stride_axis=0)

        now = turned(0)
        for k in range(n_blocks):
            later = turned(k + 1)
            hankel[b, k * LANE : (k + 1) * LANE, :] = jnp.where(keep, now, later).astype(BF16)
            now = later

    def dots(c, b):
        total = None
        cuts = 4
        step = n_blocks // 2 // cuts
        for q in reversed(range(cuts)):
            rows = n_blocks // cuts * (q + 1)
            skipped = n_blocks - rows
            part = None
            for p in range(step * q, step * (q + 1)):
                halves = []
                for half in range(2):
                    at = 2 * p + half + 1 + skipped
                    halves.append(
                        jnp.concatenate([cols_c[b, i, at : at + rows, :] for i in range(2)], axis=0).astype(BF16)
                    )
                got = jnp.dot(
                    jnp.concatenate(halves, axis=1),
                    hankel[b, 2 * LANE * p : 2 * LANE * (p + 1), :],
                    preferred_element_type=F32,
                )
                part = got if part is None else part + got
            if total is None:
                total = part
            else:
                blank = jnp.zeros((skipped, LANE), F32)
                total = total + jnp.concatenate([blank, part[:rows], blank, part[rows:]], axis=0)
        mix_out[pl.ds(c, n_blocks, stride=chans), :] = total[:n_blocks]
        filt_out[pl.ds(c, n_blocks, stride=chans), :] = total[n_blocks:]

    build(0, 0)

    def pair(i, carry):
        c = 2 * i
        build(c + 1, 1)
        dots(c, 0)
        build(jnp.minimum(c + 2, chans - 1), 0)
        dots(c + 1, 1)
        return carry

    lax.fori_loop(0, chans // 2, pair, 0)

    diagonal = iota((chans, LANE), 0) == iota((chans, LANE), 1)

    def to_lanes(x):
        return jnp.sum(jnp.where(diagonal, jnp.sum(x, axis=1, keepdims=True), 0.0), axis=0, keepdims=True)

    skip_col = jnp.sum(jnp.where(diagonal, jnp.concatenate([skip[...], jnp.zeros((1, LANE - chans), F32)], axis=1), 0.0), axis=1, keepdims=True)
    skip_sum = jnp.zeros((chans, LANE), F32)
    col_sum = jnp.zeros((chans, LANE), F32)
    flip = reversal()
    for b in range(n_blocks):
        d, half = divmod(b, 2)
        at = slice(b * chans, (b + 1) * chans)
        turned_at = slice((n_blocks - 1 - b) * chans, (n_blocks - b) * chans)
        conv = conv_s[at, :]
        mixed = jnp.dot(mix_s[at, :].astype(BF16), flip, preferred_element_type=F32)
        skip_sum = skip_sum + conv * mixed
        back[d, half * 16 : half * 16 + 16, :] = (mix_out[turned_at, :] * scale + skip_col * conv).astype(BF16)
        grad = filt_out[turned_at, :] * scale
        grad_filt[:, b * LANE : (b + 1) * LANE] = grad
        squares = grad * grad + EPS_MOMENT
        col_sum = col_sum + squares
        lag_part = jnp.sum(squares, axis=0, keepdims=True)
        if half == 0:
            first = lag_part
            continue
        tile = gain_part[:, d // 8 * LANE : (d // 8 + 1) * LANE]
        high = tile.astype(BF16).astype(F32)
        low = (tile - high).astype(BF16).astype(F32)
        rest = tile - high - low
        extra = jnp.concatenate([first, lag_part, high, low, rest, jnp.zeros((3, LANE), F32)], axis=0)
        back[d, 32:40, :] = extra.astype(BF16)
    grad_skip[...] = to_lanes(skip_sum)[:, :chans]
    mean = to_lanes(col_sum)[:, :chans] / (n_blocks * LANE)
    col_moment[...] = DECAY * col_prev[...] + (1.0 - DECAY) * mean


def finish(group, back, key, value, row_prev, grad_key, grad_value, row_moment, gain_tile):
    for half in range(key.shape[0] // LANE):
        for cb in range(key.shape[1] // LANE):
            at = (slice(half * LANE, (half + 1) * LANE), slice(cb * LANE, (cb + 1) * LANE))
            block = jnp.concatenate(
                [back[cb * 8 + d, half * 16 : half * 16 + 16, :].astype(F32) for d in range(8)], axis=0
            ).T
            grad_key[at] = (block * value[at].astype(F32)).astype(BF16)
            grad_value[at] = (block * key[at].astype(F32)).astype(BF16)
    extra = jnp.zeros((8, LANE), F32)
    for d in range(back.shape[0]):
        extra = extra + back[d, 32:40, :].astype(F32)
    lags = jnp.concatenate([extra[0:1], extra[1:2]], axis=1)
    row_moment[...] = DECAY * row_prev[...] + (1.0 - DECAY) * (lags / group)
    gain_tile[...] = extra[2:3] + extra[3:4] + extra[4:5]


def body(query, key, value, conv, cot, norm_gain, skip_gain, filters, row_prev, col_prev):
    rows, group = query.shape
    n_seq, n_ch = lax.axis_size("seq"), lax.axis_size("ch")
    chans, span = filters.shape[1:]
    n_blocks = span // LANE
    filt = filters[0]
    (sums,) = kernel_call(
        token_sums, [shape((n_ch, 2, rows), F32)], [query, conv, cot, norm_gain]
    )
    (mix_cols,) = kernel_call(mix_columns, [shape((n_seq, 32, LANE), BF16)], [key, value])
    (filt_rows,) = kernel_call(filter_rows, [shape((n_blocks * chans, LANE), BF16)], [filt])
    sums = lax.all_to_all(sums, "ch", split_axis=0, concat_axis=0, tiled=True)
    mix_cols = lax.all_to_all(mix_cols, "seq", split_axis=0, concat_axis=0, tiled=True)
    grad_query, conv_cols, gain_part = kernel_call(
        functools.partial(token_grads, group * n_ch),
        [shape((rows, group), BF16), shape((n_seq, 32, LANE), BF16), shape((1, group), F32)],
        [query, conv, cot, norm_gain, sums],
    )
    conv_cols = lax.all_to_all(conv_cols, "seq", split_axis=0, concat_axis=0, tiled=True)
    back, grad_filt, grad_skip, col_moment = kernel_call(
        functools.partial(correlations, n_blocks, 1.0 / math.sqrt(span), group),
        [
            shape((n_seq, 40, LANE), BF16),
            shape((chans, span), F32),
            shape((1, chans), F32),
            shape((1, chans), F32),
        ],
        [conv_cols, mix_cols, filt_rows, skip_gain, gain_part, col_prev],
        [
            pltpu.VMEM((n_blocks * chans, LANE), F32),
            pltpu.VMEM((n_blocks * chans, LANE), F32),
            pltpu.VMEM((n_blocks * chans, LANE), F32),
            pltpu.VMEM((2, span, LANE), BF16),
            pltpu.VMEM((2, n_blocks + 8, LANE), F32),
            pltpu.VMEM((2, 2, 2 * n_blocks, LANE), F32),
            pltpu.VMEM((n_blocks * chans, LANE), F32),
            pltpu.VMEM((n_blocks * chans, LANE), F32),
        ],
        flops=2 * chans * span * span,
    )
    back = lax.all_to_all(back, "seq", split_axis=0, concat_axis=0, tiled=True)
    grad_key, grad_value, row_moment, gain_tile = kernel_call(
        functools.partial(finish, group),
        [
            shape((rows, group), BF16),
            shape((rows, group), BF16),
            shape((1, rows), F32),
            shape((1, LANE), F32),
        ],
        [back, key, value, row_prev],
    )
    mine = lax.rem(lax.axis_index("seq"), 8) * chans
    grad_gain = lax.dynamic_slice_in_dim(gain_tile, mine, chans, axis=1)
    return grad_query, grad_key, grad_value, grad_filt[None], grad_gain, grad_skip, row_moment, col_moment


def solution(mesh):
    tokens = P("seq", "ch")
    owned = P("ch", "seq")
    spread = P("ch", "seq", None)
    return jax.shard_map(
        body,
        mesh=mesh,
        in_specs=(tokens,) * 5 + (P("ch", None), owned, spread, owned, owned),
        out_specs=(tokens,) * 3 + (spread, owned, owned, owned, owned),
        check_vma=False,
    )
```

```python
import functools
import math

import jax
import jax.numpy as jnp
from jax import lax
from jax.experimental import pallas as pl
from jax.experimental.pallas import tpu as pltpu
from jax.sharding import PartitionSpec as P

EPS_NORM = 1e-05
EPS_MOMENT = 1e-30
DECAY = 1.0 - 2.0 ** (-0.8)
F32 = jnp.float32
BF16 = jnp.bfloat16
LANE = 128


def iota(shape, axis):
    return lax.broadcasted_iota(jnp.int32, shape, axis)


STEP = 4
HALF = 64


def residue_order():
    token, lane = iota((2 * LANE, 2 * LANE), 0), iota((2 * LANE, 2 * LANE), 1)
    source = STEP * (HALF - 1 - lane % HALF) + lane // HALF
    return jnp.where(token == source, 1.0, 0.0).astype(BF16)


def kernel_call(body, outs, args, scratch=(), flops=0, in_place=(), vmem=16 << 20):
    total = sum(math.prod(a.shape) * a.dtype.itemsize for a in list(args) + list(outs))
    return pl.pallas_call(
        body,
        out_shape=tuple(outs),
        in_specs=[pl.BlockSpec(memory_space=pl.ANY if i in in_place else pltpu.VMEM) for i in range(len(args))],
        out_specs=tuple(pl.BlockSpec(memory_space=pltpu.VMEM) for _ in outs),
        scratch_shapes=list(scratch),
        compiler_params=pltpu.CompilerParams(vmem_limit_bytes=vmem),
        cost_estimate=pl.CostEstimate(flops=flops, bytes_accessed=total, transcendentals=0),
    )(*args)


def shape(dims, dtype):
    return jax.ShapeDtypeStruct(dims, dtype)


def token_sums(query_at, conv_at, cot_at, gain, out, query, conv, cot, sems):
    copies = [
        pltpu.make_async_copy(src, dst, sems.at[i])
        for i, (src, dst) in enumerate([(query_at, query), (conv_at, conv), (cot_at, cot)])
    ]
    for copy in copies:
        copy.start()
    for copy in copies:
        copy.wait()
    gated = query[...].astype(F32) * conv[...].astype(F32)
    scaled = cot[...].astype(F32) * gain[...]
    width = gated.shape[1]

    def fold(x):
        part = sum(x[:, k : k + LANE] for k in range(0, width, LANE))
        cols = [
            jnp.sum(part[r : r + LANE].T, axis=0, keepdims=True) for r in range(0, part.shape[0], LANE)
        ]
        return jnp.concatenate(cols, axis=1)

    both = jnp.concatenate([fold(gated * gated), fold(scaled * gated)], axis=0)
    for peer in range(out.shape[0]):
        out[peer] = both


def mix_columns(key, value, out):
    mixed = (key[...].astype(F32) * value[...].astype(F32)).astype(BF16).astype(F32)
    order = residue_order()
    for cb in range(mixed.shape[1] // LANE):
        block = mixed[:, cb * LANE : (cb + 1) * LANE].T.astype(BF16)
        block = jnp.dot(block, order, preferred_element_type=F32).astype(BF16)
        for d in range(8):
            for tile in range(2):
                out[cb * 8 + d, tile * 16 : tile * 16 + 16, :] = block[
                    d * 16 : d * 16 + 16, tile * LANE : (tile + 1) * LANE
                ]


def filter_rows(filt, out):
    order = residue_order()
    for n in range(filt.shape[1] // (2 * LANE)):
        block = filt[:, n * 2 * LANE : (n + 1) * 2 * LANE].astype(BF16)
        block = jnp.dot(block, order, preferred_element_type=F32).astype(BF16)
        for tile in range(2):
            out[n, tile * 16 : tile * 16 + 16, :] = block[:, tile * LANE : (tile + 1) * LANE]


def token_grads(total_width, query, conv, cot, gain, near, far, mix_cols, grad_query, cols, gain_part):
    totals = near[...] + far[...]
    inv_row = lax.rsqrt(totals[0:1, :] / total_width + EPS_NORM)
    back_row = inv_row * inv_row * (totals[1:2, :] / total_width)
    rows = query.shape[0]
    cols[:, 32:64, :] = mix_cols[...]
    both = jnp.concatenate([inv_row, back_row, jnp.zeros((6, rows), F32)], axis=0)
    for half in range(rows // LANE):
        lo = half * LANE
        turned = jnp.concatenate([both[:, lo : lo + LANE]] * (LANE // 8), axis=0).T
        inv = turned[:, 0:1]
        back = turned[:, 1:2]
        for cb in range(query.shape[1] // LANE):
            at = (slice(lo, lo + LANE), slice(cb * LANE, (cb + 1) * LANE))
            query32 = query[at].astype(F32)
            conv32 = conv[at].astype(F32)
            cot32 = cot[at].astype(F32)
            gated = query32 * conv32
            grad = inv * (cot32 * gain[:, at[1]] - gated * back)
            grad_query[at] = (grad * conv32).astype(BF16)
            block = (grad * query32).T.astype(BF16)
            for d in range(8):
                cols[cb * 8 + d, half * 16 : half * 16 + 16, :] = block[d * 16 : d * 16 + 16, :]
            part = jnp.sum(cot32 * gated * inv, axis=0, keepdims=True)
            if half == 0:
                gain_part[:, at[1]] = part
            else:
                gain_part[:, at[1]] += part


def correlations(
    scale, cols, filt, skip, gain_part, col_prev,
    back, grad_filt, grad_skip, col_moment,
    conv_s, wide_s, hankel, conv_c, wide_c, mix_out, filt_out,
):
    chans = 16
    peers = cols.shape[0]
    n_tiles = 2 * peers
    segments = 2 * STEP
    lead = 8
    lane = iota((chans, LANE), 1)
    rows_kept = iota((32, LANE), 1) < STEP + STEP * iota((32, LANE), 0)

    def residues(ref, n, first):
        if n < 0 or n >= peers:
            return [jnp.zeros((chans, LANE), F32)] * 2
        return [ref[n, first + tile * 16 : first + tile * 16 + 16, :].astype(F32) for tile in range(2)]

    for d in range(peers):
        conv_s[d * 32 : d * 32 + 32, :] = cols[d, 0:32, :].astype(F32)
    for which, (ref, first) in enumerate([(filt, 0), (cols, 32)]):
        for r in range(STEP):
            wide_s[which * STEP + r, 0 : lead * chans, :] = jnp.zeros((lead * chans, LANE), F32)
        now = residues(ref, -1, first)
        now_rolled = now
        for n in range(-1, peers - 1):
            later = residues(ref, n + 1, first)
            later_rolled = [pltpu.roll(x, HALF, axis=1) for x in later]
            at = slice((lead + n) * chans, (lead + n + 1) * chans)
            for tile in range(2):
                low = which * STEP + 2 * tile
                wide_s[low, at, :] = jnp.where(lane < HALF, now[tile], later_rolled[tile])
                wide_s[low + 1, at, :] = jnp.where(lane < HALF, now_rolled[tile], later[tile])
            now, now_rolled = later, later_rolled
    for b in range(2):
        hankel[b, n_tiles * 32 : (n_tiles + 1) * 32, :] = jnp.zeros((32, LANE), BF16)
        for seg in range(segments):
            wide_c[b, seg, 0 : peers - lead, :] = jnp.zeros((peers - lead, LANE), F32)

    def build(c, b):
        conv_c[b] = conv_s[pl.ds(c, n_tiles, stride=chans), :]
        for seg in range(segments):
            wide_c[b, seg, peers - lead : 2 * peers, :] = wide_s[seg, pl.ds(c, peers + lead, stride=chans), :]

        def turned(k):
            if k == n_tiles:
                return jnp.zeros((32, LANE), F32)
            wide = jnp.broadcast_to(conv_c[b, k : k + 1, :], (32, LANE))
            return pltpu.roll(wide, STEP, axis=1, stride=STEP, stride_axis=0)

        now = turned(0)
        for k in range(n_tiles):
            later = turned(k + 1)
            hankel[b, k * 32 : (k + 1) * 32, :] = jnp.where(rows_kept, now, later).astype(BF16)
            now = later

    def dots(c, b):
        cuts = 4
        total = None
        for q in reversed(range(cuts)):
            rows = peers // cuts * (q + 1)
            skipped = peers - rows
            part = None
            for n in range(peers // cuts * q, peers // cuts * (q + 1), 4):
                left = []
                for half in range(2):
                    at = n + 2 * half + 1 + skipped
                    left.append(
                        jnp.concatenate([wide_c[b, seg, at : at + rows, :] for seg in range(segments)], axis=0).astype(BF16)
                    )
                right = []
                for k in range(2 * n, 2 * n + 8, 2):
                    for t in (k + 1, k):
                        right.append(
                            jnp.concatenate([hankel[b, 32 * t : 32 * t + 32, :], hankel[b, 32 * t + 32 : 32 * t + 64, :]], axis=1)
                        )
                got = jnp.dot(
                    jnp.concatenate(left, axis=1), jnp.concatenate(right, axis=0), preferred_element_type=F32
                )
                part = got if part is None else part + got
            pieces = [part[seg * rows : (seg + 1) * rows] for seg in range(segments)]
            if total is None:
                total = pieces
            else:
                blank = jnp.zeros((skipped, 2 * LANE), F32)
                total = [x + jnp.concatenate([blank, y], axis=0) for x, y in zip(total, pieces)]

        inner = iota((peers, LANE), 1) < LANE - 1
        top = jnp.zeros((1, LANE), F32)

        def later_by_one(x):
            first, second = [pltpu.roll(x[:, t * LANE : (t + 1) * LANE], LANE - 1, axis=1) for t in range(2)]
            below = jnp.concatenate([top, first[:-1]], axis=0)
            return jnp.concatenate([jnp.where(inner, first, second), jnp.where(inner, second, below)], axis=1)

        for which, out in enumerate([mix_out, filt_out]):
            sums = total[which * STEP + STEP - 1]
            for r in reversed(range(STEP - 1)):
                sums = total[which * STEP + r] + later_by_one(sums)
            for tile in range(2):
                out[tile, pl.ds(c, peers, stride=chans), :] = sums[:, tile * LANE : (tile + 1) * LANE]

    build(0, 0)

    def pair(i, carry):
        c = 2 * i
        build(c + 1, 1)
        dots(c, 0)
        build(jnp.minimum(c + 2, chans - 1), 0)
        dots(c + 1, 1)
        return carry

    lax.fori_loop(0, chans // 2, pair, 0)

    diagonal = iota((chans, LANE), 0) == iota((chans, LANE), 1)

    def to_lanes(x):
        return jnp.sum(jnp.where(diagonal, x, 0.0), axis=0, keepdims=True)

    skip_col = jnp.sum(
        jnp.where(diagonal, jnp.concatenate([skip[...], jnp.zeros((1, LANE - chans), F32)], axis=1), 0.0),
        axis=1,
        keepdims=True,
    )
    col_sum = jnp.zeros((chans, LANE), F32)
    for d in range(peers):
        at = slice((peers - 1 - d) * chans, (peers - d) * chans)
        lags = []
        for tile in range(2):
            k = 2 * d + tile
            conv = conv_s[k * chans : (k + 1) * chans, :]
            back[d, tile * 16 : tile * 16 + 16, :] = (mix_out[tile, at, :] * scale + skip_col * conv).astype(BF16)
            grad = filt_out[tile, at, :] * scale
            grad_filt[:, k * LANE : (k + 1) * LANE] = grad
            squares = grad * grad + EPS_MOMENT
            col_sum = col_sum + squares
            lags.append(jnp.sum(squares, axis=0, keepdims=True))
        part = gain_part[:, d // 8 * LANE : (d // 8 + 1) * LANE]
        high = part.astype(BF16).astype(F32)
        low = (part - high).astype(BF16).astype(F32)
        extra = jnp.concatenate(lags + [high, low, part - high - low, jnp.zeros((3, LANE), F32)], axis=0)
        back[d, 32:40, :] = extra.astype(BF16)
    grad_skip[...] = to_lanes(filt_out[0, (peers - 1) * chans : peers * chans, 0:1])[:, :chans]
    mean = to_lanes(jnp.sum(col_sum, axis=1, keepdims=True))[:, :chans] / (n_tiles * LANE)
    col_moment[...] = DECAY * col_prev[...] + (1.0 - DECAY) * mean


def finish(group, back, key, value, row_prev, grad_key, grad_value, row_moment, grad_gain):
    for half in range(key.shape[0] // LANE):
        for cb in range(key.shape[1] // LANE):
            at = (slice(half * LANE, (half + 1) * LANE), slice(cb * LANE, (cb + 1) * LANE))
            block = jnp.concatenate(
                [back[cb * 8 + d, half * 16 : half * 16 + 16, :].astype(F32) for d in range(8)], axis=0
            ).T
            grad_key[at] = (block * value[at].astype(F32)).astype(BF16)
            grad_value[at] = (block * key[at].astype(F32)).astype(BF16)
    extra = jnp.zeros((8, LANE), F32)
    for d in range(back.shape[0]):
        extra = extra + back[d, 32:40, :].astype(F32)
    lags = jnp.concatenate([extra[0:1], extra[1:2]], axis=1)
    row_moment[...] = DECAY * row_prev[...] + (1.0 - DECAY) * (lags / group)
    gains = jnp.broadcast_to(extra[2:3] + extra[3:4] + extra[4:5], (8, LANE))
    chans = grad_gain.shape[1]
    place = lax.rem(lax.axis_index("seq"), LANE // chans)
    grad_gain[...] = pltpu.roll(gains, lax.rem(LANE - place * chans, LANE), axis=1)[0:1, :chans]


def sum_over_channels(sums):
    groups = [[4 * x + 2 * z + core for x in range(4) for core in range(2)] for z in range(2)]
    parts = lax.all_to_all(sums, "ch", split_axis=0, concat_axis=0, axis_index_groups=groups, tiled=True)
    here = jnp.sum(parts, axis=0)
    return here, lax.ppermute(here, "ch", [(i, i ^ 2) for i in range(16)])


def correlate_call(chans, span, peers, args):
    return kernel_call(
        functools.partial(correlations, 1.0 / math.sqrt(span)),
        [
            shape((peers, 40, LANE), BF16),
            shape((chans, span), F32),
            shape((1, chans), F32),
            shape((1, chans), F32),
        ],
        args,
        [
            pltpu.VMEM((2 * peers * chans, LANE), F32),
            pltpu.VMEM((2 * STEP, (peers + 8) * chans, LANE), F32),
            pltpu.VMEM((2, (2 * peers + 1) * 32, LANE), BF16),
            pltpu.VMEM((2, 2 * peers, LANE), F32),
            pltpu.VMEM((2, 2 * STEP, 2 * peers, LANE), F32),
            pltpu.VMEM((2, peers * chans, LANE), F32),
            pltpu.VMEM((2, peers * chans, LANE), F32),
        ],
        flops=2 * chans * span * span,
        vmem=40 << 20,
    )


def body(query, key, value, conv, cot, norm_gain, skip_gain, filters, row_prev, col_prev):
    rows, group = query.shape
    n_seq, n_ch = lax.axis_size("seq"), lax.axis_size("ch")
    chans, span = filters.shape[1:]
    (sums,) = kernel_call(
        token_sums,
        [shape((n_ch // 2, 2, rows), F32)],
        [query, conv, cot, norm_gain],
        [pltpu.VMEM((rows, group), BF16)] * 3 + [pltpu.SemaphoreType.DMA((3,))],
        in_place=(0, 1, 2),
        vmem=60 << 20,
    )
    (mix_cols,) = kernel_call(mix_columns, [shape((n_seq, 32, LANE), BF16)], [key, value])
    (filt_rows,) = kernel_call(filter_rows, [shape((n_seq, 32, LANE), BF16)], [filters[0]])
    near, far = sum_over_channels(sums)
    grad_query, cols, gain_part = kernel_call(
        functools.partial(token_grads, group * n_ch),
        [shape((rows, group), BF16), shape((n_seq, 64, LANE), BF16), shape((1, group), F32)],
        [query, conv, cot, norm_gain, near, far, mix_cols],
    )
    cols = lax.all_to_all(cols, "seq", split_axis=0, concat_axis=0, tiled=True)
    back, grad_filt, grad_skip, col_moment = correlate_call(
        chans, span, n_seq, [cols, filt_rows, skip_gain, gain_part, col_prev]
    )
    back = lax.all_to_all(back, "seq", split_axis=0, concat_axis=0, tiled=True)
    grad_key, grad_value, row_moment, grad_gain = kernel_call(
        functools.partial(finish, group),
        [
            shape((rows, group), BF16),
            shape((rows, group), BF16),
            shape((1, rows), F32),
            shape((1, chans), F32),
        ],
        [back, key, value, row_prev],
    )
    return grad_query, grad_key, grad_value, grad_filt[None], grad_gain, grad_skip, row_moment, col_moment


def solution(mesh):
    tokens = P("seq", "ch")
    owned = P("ch", "seq")
    spread = P("ch", "seq", None)
    return jax.shard_map(
        body,
        mesh=mesh,
        in_specs=(tokens,) * 5 + (P("ch", None), owned, spread, owned, owned),
        out_specs=(tokens,) * 3 + (spread, owned, owned, owned, owned),
        check_vma=False,
    )
```

```python
import functools
import itertools
import math

import jax
import jax.numpy as jnp
from jax import lax
from jax.experimental import pallas as pl
from jax.experimental.pallas import tpu as pltpu
from jax.sharding import PartitionSpec as P

EPS_NORM = 1e-05
EPS_MOMENT = 1e-30
DECAY = 1.0 - 2.0 ** (-0.8)
F32 = jnp.float32
BF16 = jnp.bfloat16
LANE = 128


def iota(shape, axis):
    return lax.broadcasted_iota(jnp.int32, shape, axis)


STEP = 4
HALF = 64


def residue_order():
    token, lane = iota((2 * LANE, 2 * LANE), 0), iota((2 * LANE, 2 * LANE), 1)
    source = STEP * (HALF - 1 - lane % HALF) + lane // HALF
    return jnp.where(token == source, 1.0, 0.0).astype(BF16)


def kernel_call(body, outs, args, scratch=(), flops=0, in_place=(), vmem=16 << 20):
    total = sum(math.prod(a.shape) * a.dtype.itemsize for a in list(args) + list(outs))
    return pl.pallas_call(
        body,
        out_shape=tuple(outs),
        in_specs=[pl.BlockSpec(memory_space=pl.ANY if i in in_place else pltpu.VMEM) for i in range(len(args))],
        out_specs=tuple(pl.BlockSpec(memory_space=pltpu.VMEM) for _ in outs),
        scratch_shapes=list(scratch),
        compiler_params=pltpu.CompilerParams(vmem_limit_bytes=vmem),
        cost_estimate=pl.CostEstimate(flops=flops, bytes_accessed=total, transcendentals=0),
    )(*args)


def shape(dims, dtype):
    return jax.ShapeDtypeStruct(dims, dtype)


def token_sums(query_at, conv_at, cot_at, gain_at, out, query, conv, cot, gain, sems):
    rows, width = query.shape
    pairs = [(query_at, query), (conv_at, conv), (cot_at, cot)]
    copies = []
    gain_copy = pltpu.make_async_copy(gain_at, gain, sems.at[rows // LANE, 0])
    gain_copy.start()
    for r in range(rows // LANE):
        at = pl.ds(r * LANE, LANE)
        copies.append([pltpu.make_async_copy(x.at[at], y.at[at], sems.at[r, i]) for i, (x, y) in enumerate(pairs)])
        for copy in copies[-1]:
            copy.start()
    gain_copy.wait()
    gain_row = gain[...]
    for r in range(rows // LANE):
        for copy in copies[r]:
            copy.wait()
        at = slice(r * LANE, (r + 1) * LANE)
        square = jnp.zeros((LANE, LANE), F32)
        dot = jnp.zeros((LANE, LANE), F32)
        for k in range(0, width, LANE):
            gated = query[at, k : k + LANE].astype(F32) * conv[at, k : k + LANE].astype(F32)
            square = square + gated * gated
            dot = dot + cot[at, k : k + LANE].astype(F32) * gain_row[:, k : k + LANE] * gated
        both = jnp.concatenate([jnp.sum(x.T, axis=0, keepdims=True) for x in (square, dot)], axis=0)
        for peer in range(out.shape[0]):
            out[peer, :, at] = both


def mix_columns(key, value, out):
    mixed = (key[...].astype(F32) * value[...].astype(F32)).astype(BF16).astype(F32)
    order = residue_order()
    for cb in range(mixed.shape[1] // LANE):
        block = mixed[:, cb * LANE : (cb + 1) * LANE].T.astype(BF16)
        block = jnp.dot(block, order, preferred_element_type=F32).astype(BF16)
        for d in range(8):
            for tile in range(2):
                out[cb * 8 + d, tile * 16 : tile * 16 + 16, :] = block[
                    d * 16 : d * 16 + 16, tile * LANE : (tile + 1) * LANE
                ]


def filter_rows(filt, out):
    order = residue_order()
    for n in range(filt.shape[1] // (2 * LANE)):
        block = filt[:, n * 2 * LANE : (n + 1) * 2 * LANE].astype(BF16)
        block = jnp.dot(block, order, preferred_element_type=F32).astype(BF16)
        for tile in range(2):
            out[n, tile * 16 : tile * 16 + 16, :] = block[:, tile * LANE : (tile + 1) * LANE]


def turned_products(query, conv, cot, gain, plain, gated_q):
    for half in range(query.shape[0] // LANE):
        for cb in range(query.shape[1] // LANE):
            at = (slice(half * LANE, (half + 1) * LANE), slice(cb * LANE, (cb + 1) * LANE))
            to = (slice(cb * LANE, (cb + 1) * LANE), slice(half * LANE, (half + 1) * LANE))
            query32 = query[at].astype(F32)
            plain[to] = (cot[at].astype(F32) * gain[:, at[1]] * query32).T
            gated_q[to] = (query32 * conv[at].astype(F32) * query32).T


def token_scales(total_width, near, far):
    totals = near[...] + far[...]
    inv = lax.rsqrt(totals[0:1, :] / total_width + EPS_NORM)
    return inv, inv * inv * (totals[1:2, :] / total_width)


def send_columns(total_width, plain, gated_q, near, far, mix_cols, cols):
    inv, back = token_scales(total_width, near, far)
    cols[:, 32:64, :] = mix_cols[...]
    for half in range(plain.shape[1] // LANE):
        lo = slice(half * LANE, (half + 1) * LANE)
        for d in range(cols.shape[0]):
            at = (slice(d * 16, d * 16 + 16), lo)
            grad = inv[:, lo] * (plain[at] - back[:, lo] * gated_q[at])
            cols[d, half * 16 : half * 16 + 16, :] = grad.astype(BF16)


def token_grads(total_width, query, conv, cot, gain, near, far, grad_query, gain_part):
    rows = query.shape[0]
    inv_row, back_row = token_scales(total_width, near, far)
    both = jnp.concatenate([inv_row, back_row, jnp.zeros((6, rows), F32)], axis=0)
    for half in range(rows // LANE):
        lo = half * LANE
        turned = jnp.concatenate([both[:, lo : lo + LANE]] * (LANE // 8), axis=0).T
        inv = turned[:, 0:1]
        back = turned[:, 1:2]
        for cb in range(query.shape[1] // LANE):
            at = (slice(lo, lo + LANE), slice(cb * LANE, (cb + 1) * LANE))
            conv32 = conv[at].astype(F32)
            cot32 = cot[at].astype(F32)
            gated = query[at].astype(F32) * conv32
            grad = inv * (cot32 * gain[:, at[1]] - gated * back)
            grad_query[at] = (grad * conv32).astype(BF16)
            part = jnp.sum(cot32 * gated * inv, axis=0, keepdims=True)
            if half == 0:
                gain_part[:, at[1]] = part
            else:
                gain_part[:, at[1]] += part


def correlations(
    scale, cols, filt, skip, gain_part, col_prev,
    back, grad_filt, grad_skip, col_moment,
    conv_s, wide_s, hankel, conv_c, wide_c, mix_out, filt_out,
):
    chans = 16
    peers = cols.shape[0]
    n_tiles = 2 * peers
    segments = 2 * STEP
    lead = 8
    lane = iota((chans, LANE), 1)
    rows_kept = iota((32, LANE), 1) < STEP + STEP * iota((32, LANE), 0)

    def residues(ref, n, first):
        if n < 0 or n >= peers:
            return [jnp.zeros((chans, LANE), F32)] * 2
        return [ref[n, first + tile * 16 : first + tile * 16 + 16, :].astype(F32) for tile in range(2)]

    for d in range(peers):
        conv_s[d * 32 : d * 32 + 32, :] = cols[d, 0:32, :].astype(F32)
    for which, (ref, first) in enumerate([(filt, 0), (cols, 32)]):
        for r in range(STEP):
            wide_s[which * STEP + r, 0 : lead * chans, :] = jnp.zeros((lead * chans, LANE), F32)
        now = residues(ref, -1, first)
        now_rolled = now
        for n in range(-1, peers - 1):
            later = residues(ref, n + 1, first)
            later_rolled = [pltpu.roll(x, HALF, axis=1) for x in later]
            at = slice((lead + n) * chans, (lead + n + 1) * chans)
            for tile in range(2):
                low = which * STEP + 2 * tile
                wide_s[low, at, :] = jnp.where(lane < HALF, now[tile], later_rolled[tile])
                wide_s[low + 1, at, :] = jnp.where(lane < HALF, now_rolled[tile], later[tile])
            now, now_rolled = later, later_rolled
    for b in range(4):
        hankel[b, n_tiles * 32 : (n_tiles + 1) * 32, :] = jnp.zeros((32, LANE), BF16)
        for seg in range(segments):
            wide_c[b, seg, 0 : peers - lead, :] = jnp.zeros((peers - lead, LANE), F32)

    def build(c, b):
        conv_c[b] = conv_s[pl.ds(c, n_tiles, stride=chans), :]
        for seg in range(segments):
            wide_c[b, seg, peers - lead : 2 * peers, :] = wide_s[seg, pl.ds(c, peers + lead, stride=chans), :]

        def turned(k):
            if k == n_tiles:
                return jnp.zeros((32, LANE), F32)
            wide = jnp.broadcast_to(conv_c[b, k : k + 1, :], (32, LANE))
            return pltpu.roll(wide, STEP, axis=1, stride=STEP, stride_axis=0)

        now = turned(0)
        for k in range(n_tiles):
            later = turned(k + 1)
            hankel[b, k * 32 : (k + 1) * 32, :] = jnp.where(rows_kept, now, later).astype(BF16)
            now = later
            if k % 16 == 15:
                yield

    def dots(c, b):
        cuts = 4
        total = None
        for q in reversed(range(cuts)):
            rows = peers // cuts * (q + 1)
            skipped = peers - rows
            left, right = [], []
            for n in range(peers // cuts * q, peers // cuts * (q + 1), 4):
                for half in range(2):
                    at = n + 2 * half + 1 + skipped
                    left.append(
                        jnp.concatenate([wide_c[b, seg, at : at + rows, :] for seg in range(segments)], axis=0).astype(BF16)
                    )
                for k in range(2 * n, 2 * n + 8, 2):
                    for t in (k + 1, k):
                        right.append(
                            jnp.concatenate([hankel[b, 32 * t : 32 * t + 32, :], hankel[b, 32 * t + 32 : 32 * t + 64, :]], axis=1)
                        )
            part = jnp.dot(
                jnp.concatenate(left, axis=1), jnp.concatenate(right, axis=0), preferred_element_type=F32
            )
            yield
            pieces = [part[seg * rows : (seg + 1) * rows] for seg in range(segments)]
            if total is None:
                total = pieces
            else:
                blank = jnp.zeros((skipped, 2 * LANE), F32)
                total = [x + jnp.concatenate([blank, y], axis=0) for x, y in zip(total, pieces)]

        inner = iota((peers, LANE), 1) < LANE - 1
        top = jnp.zeros((1, LANE), F32)

        def later_by_one(x):
            first, second = [pltpu.roll(x[:, t * LANE : (t + 1) * LANE], LANE - 1, axis=1) for t in range(2)]
            below = jnp.concatenate([top, first[:-1]], axis=0)
            return jnp.concatenate([jnp.where(inner, first, second), jnp.where(inner, second, below)], axis=1)

        for which, out in enumerate([mix_out, filt_out]):
            sums = total[which * STEP + STEP - 1]
            for r in reversed(range(STEP - 1)):
                sums = total[which * STEP + r] + later_by_one(sums)
            for tile in range(2):
                out[tile, pl.ds(c, peers, stride=chans), :] = sums[:, tile * LANE : (tile + 1) * LANE]

    def together(*steps):
        for _ in itertools.zip_longest(*steps):
            pass

    together(build(0, 0), build(1, 1))

    def four(i, carry):
        c = 4 * i
        together(build(c + 2, 2), build(c + 3, 3), dots(c, 0), dots(c + 1, 1))
        together(build(jnp.minimum(c + 4, chans - 2), 0), build(jnp.minimum(c + 5, chans - 1), 1), dots(c + 2, 2), dots(c + 3, 3))
        return carry

    lax.fori_loop(0, chans // 4, four, 0)

    diagonal = iota((chans, LANE), 0) == iota((chans, LANE), 1)

    def to_lanes(x):
        return jnp.sum(jnp.where(diagonal, x, 0.0), axis=0, keepdims=True)

    skip_col = jnp.sum(
        jnp.where(diagonal, jnp.concatenate([skip[...], jnp.zeros((1, LANE - chans), F32)], axis=1), 0.0),
        axis=1,
        keepdims=True,
    )
    col_sum = jnp.zeros((chans, LANE), F32)
    for d in range(peers):
        at = slice((peers - 1 - d) * chans, (peers - d) * chans)
        lags = []
        for tile in range(2):
            k = 2 * d + tile
            conv = conv_s[k * chans : (k + 1) * chans, :]
            back[d, tile * 16 : tile * 16 + 16, :] = (mix_out[tile, at, :] * scale + skip_col * conv).astype(BF16)
            grad = filt_out[tile, at, :] * scale
            grad_filt[:, k * LANE : (k + 1) * LANE] = grad
            squares = grad * grad + EPS_MOMENT
            col_sum = col_sum + squares
            lags.append(jnp.sum(squares, axis=0, keepdims=True))
        part = gain_part[:, d // 8 * LANE : (d // 8 + 1) * LANE]
        high = part.astype(BF16).astype(F32)
        low = (part - high).astype(BF16).astype(F32)
        extra = jnp.concatenate(lags + [high, low, part - high - low, jnp.zeros((3, LANE), F32)], axis=0)
        back[d, 32:40, :] = extra.astype(BF16)
    grad_skip[...] = to_lanes(filt_out[0, (peers - 1) * chans : peers * chans, 0:1])[:, :chans]
    mean = to_lanes(jnp.sum(col_sum, axis=1, keepdims=True))[:, :chans] / (n_tiles * LANE)
    col_moment[...] = DECAY * col_prev[...] + (1.0 - DECAY) * mean


def finish(group, back, key, value, row_prev, grad_key, grad_value, row_moment, grad_gain):
    for half in range(key.shape[0] // LANE):
        for cb in range(key.shape[1] // LANE):
            at = (slice(half * LANE, (half + 1) * LANE), slice(cb * LANE, (cb + 1) * LANE))
            block = jnp.concatenate(
                [back[cb * 8 + d, half * 16 : half * 16 + 16, :].astype(F32) for d in range(8)], axis=0
            ).T
            grad_key[at] = (block * value[at].astype(F32)).astype(BF16)
            grad_value[at] = (block * key[at].astype(F32)).astype(BF16)
    extra = jnp.zeros((8, LANE), F32)
    for d in range(back.shape[0]):
        extra = extra + back[d, 32:40, :].astype(F32)
    lags = jnp.concatenate([extra[0:1], extra[1:2]], axis=1)
    row_moment[...] = DECAY * row_prev[...] + (1.0 - DECAY) * (lags / group)
    gains = jnp.broadcast_to(extra[2:3] + extra[3:4] + extra[4:5], (8, LANE))
    chans = grad_gain.shape[1]
    place = lax.rem(lax.axis_index("seq"), LANE // chans)
    grad_gain[...] = pltpu.roll(gains, lax.rem(LANE - place * chans, LANE), axis=1)[0:1, :chans]


def sum_over_channels(sums):
    groups = [[4 * x + 2 * z + core for x in range(4) for core in range(2)] for z in range(2)]
    parts = lax.all_to_all(sums, "ch", split_axis=0, concat_axis=0, axis_index_groups=groups, tiled=True)
    here = jnp.sum(parts, axis=0)
    return here, lax.ppermute(here, "ch", [(i, i ^ 2) for i in range(16)])


def correlate_call(chans, span, peers, args):
    return kernel_call(
        functools.partial(correlations, 1.0 / math.sqrt(span)),
        [
            shape((peers, 40, LANE), BF16),
            shape((chans, span), F32),
            shape((1, chans), F32),
            shape((1, chans), F32),
        ],
        args,
        [
            pltpu.VMEM((2 * peers * chans, LANE), F32),
            pltpu.VMEM((2 * STEP, (peers + 8) * chans, LANE), F32),
            pltpu.VMEM((4, (2 * peers + 1) * 32, LANE), BF16),
            pltpu.VMEM((4, 2 * peers, LANE), F32),
            pltpu.VMEM((4, 2 * STEP, 2 * peers, LANE), F32),
            pltpu.VMEM((2, peers * chans, LANE), F32),
            pltpu.VMEM((2, peers * chans, LANE), F32),
        ],
        flops=2 * chans * span * span,
        vmem=40 << 20,
    )


def body(query, key, value, conv, cot, norm_gain, skip_gain, filters, row_prev, col_prev):
    rows, group = query.shape
    n_seq, n_ch = lax.axis_size("seq"), lax.axis_size("ch")
    chans, span = filters.shape[1:]
    (sums,) = kernel_call(
        token_sums,
        [shape((n_ch // 2, 2, rows), F32)],
        [query, conv, cot, norm_gain],
        [pltpu.VMEM((rows, group), BF16)] * 3
        + [pltpu.VMEM((1, group), F32), pltpu.SemaphoreType.DMA((rows // LANE + 1, 3))],
        in_place=(0, 1, 2, 3),
        vmem=60 << 20,
    )
    (mix_cols,) = kernel_call(mix_columns, [shape((n_seq, 32, LANE), BF16)], [key, value])
    (filt_rows,) = kernel_call(filter_rows, [shape((n_seq, 32, LANE), BF16)], [filters[0]])
    near, far = sum_over_channels(sums)
    plain, gated_q = kernel_call(
        turned_products, [shape((group, rows), F32)] * 2, [query, conv, cot, norm_gain]
    )
    (cols,) = kernel_call(
        functools.partial(send_columns, group * n_ch),
        [shape((n_seq, 64, LANE), BF16)],
        [plain, gated_q, near, far, mix_cols],
    )
    grad_query, gain_part = kernel_call(
        functools.partial(token_grads, group * n_ch),
        [shape((rows, group), BF16), shape((1, group), F32)],
        [query, conv, cot, norm_gain, near, far],
    )
    cols = lax.all_to_all(cols, "seq", split_axis=0, concat_axis=0, tiled=True)
    back, grad_filt, grad_skip, col_moment = correlate_call(
        chans, span, n_seq, [cols, filt_rows, skip_gain, gain_part, col_prev]
    )
    back = lax.all_to_all(back, "seq", split_axis=0, concat_axis=0, tiled=True)
    grad_key, grad_value, row_moment, grad_gain = kernel_call(
        functools.partial(finish, group),
        [
            shape((rows, group), BF16),
            shape((rows, group), BF16),
            shape((1, rows), F32),
            shape((1, chans), F32),
        ],
        [back, key, value, row_prev],
    )
    return grad_query, grad_key, grad_value, grad_filt[None], grad_gain, grad_skip, row_moment, col_moment


def solution(mesh):
    tokens = P("seq", "ch")
    owned = P("ch", "seq")
    spread = P("ch", "seq", None)
    return jax.shard_map(
        body,
        mesh=mesh,
        in_specs=(tokens,) * 5 + (P("ch", None), owned, spread, owned, owned),
        out_specs=(tokens,) * 3 + (spread, owned, owned, owned, owned),
        check_vma=False,
    )
```

```python
import functools
import itertools
import math

import jax
import jax.numpy as jnp
from jax import lax
from jax.experimental import pallas as pl
from jax.experimental.pallas import tpu as pltpu
from jax.sharding import PartitionSpec as P

EPS_NORM = 1e-05
EPS_MOMENT = 1e-30
DECAY = 1.0 - 2.0 ** (-0.8)
F32 = jnp.float32
BF16 = jnp.bfloat16
LANE = 128


def iota(shape, axis):
    return lax.broadcasted_iota(jnp.int32, shape, axis)


STEP = 4
HALF = 64


def residue_order():
    token, lane = iota((2 * LANE, 2 * LANE), 0), iota((2 * LANE, 2 * LANE), 1)
    source = STEP * (HALF - 1 - lane % HALF) + lane // HALF
    return jnp.where(token == source, 1.0, 0.0).astype(BF16)


def kernel_call(body, outs, args, scratch=(), flops=0, in_place=(), vmem=16 << 20):
    total = sum(math.prod(a.shape) * a.dtype.itemsize for a in list(args) + list(outs))
    return pl.pallas_call(
        body,
        out_shape=tuple(outs),
        in_specs=[pl.BlockSpec(memory_space=pl.ANY if i in in_place else pltpu.VMEM) for i in range(len(args))],
        out_specs=tuple(pl.BlockSpec(memory_space=pltpu.VMEM) for _ in outs),
        scratch_shapes=list(scratch),
        compiler_params=pltpu.CompilerParams(vmem_limit_bytes=vmem),
        cost_estimate=pl.CostEstimate(flops=flops, bytes_accessed=total, transcendentals=0),
    )(*args)


def shape(dims, dtype):
    return jax.ShapeDtypeStruct(dims, dtype)


def token_sums(query_at, conv_at, cot_at, gain_at, out, query, conv, cot, gain, sems):
    rows, width = query.shape
    pairs = [(query_at, query), (conv_at, conv), (cot_at, cot)]
    copies = []
    gain_copy = pltpu.make_async_copy(gain_at, gain, sems.at[rows // LANE, 0])
    gain_copy.start()
    for r in range(rows // LANE):
        at = pl.ds(r * LANE, LANE)
        copies.append([pltpu.make_async_copy(x.at[at], y.at[at], sems.at[r, i]) for i, (x, y) in enumerate(pairs)])
        for copy in copies[-1]:
            copy.start()
    gain_copy.wait()
    gain_row = gain[...]
    for r in range(rows // LANE):
        for copy in copies[r]:
            copy.wait()
        at = slice(r * LANE, (r + 1) * LANE)
        square = jnp.zeros((LANE, LANE), F32)
        dot = jnp.zeros((LANE, LANE), F32)
        for k in range(0, width, LANE):
            gated = query[at, k : k + LANE].astype(F32) * conv[at, k : k + LANE].astype(F32)
            square = square + gated * gated
            dot = dot + cot[at, k : k + LANE].astype(F32) * gain_row[:, k : k + LANE] * gated
        both = jnp.concatenate([jnp.sum(x.T, axis=0, keepdims=True) for x in (square, dot)], axis=0)
        for peer in range(out.shape[0]):
            out[peer, :, at] = both


def mix_columns(key, value, out):
    mixed = (key[...].astype(F32) * value[...].astype(F32)).astype(BF16).astype(F32)
    order = residue_order()
    for cb in range(mixed.shape[1] // LANE):
        block = mixed[:, cb * LANE : (cb + 1) * LANE].T.astype(BF16)
        block = jnp.dot(block, order, preferred_element_type=F32).astype(BF16)
        for d in range(8):
            for tile in range(2):
                out[cb * 8 + d, tile * 16 : tile * 16 + 16, :] = block[
                    d * 16 : d * 16 + 16, tile * LANE : (tile + 1) * LANE
                ]


def filter_rows(filt, out):
    order = residue_order()
    for n in range(filt.shape[1] // (2 * LANE)):
        block = filt[:, n * 2 * LANE : (n + 1) * 2 * LANE].astype(BF16)
        block = jnp.dot(block, order, preferred_element_type=F32).astype(BF16)
        for tile in range(2):
            out[n, tile * 16 : tile * 16 + 16, :] = block[:, tile * LANE : (tile + 1) * LANE]


def turned_products(query, conv, cot, gain, plain, gated_q):
    for half in range(query.shape[0] // LANE):
        for cb in range(query.shape[1] // LANE):
            at = (slice(half * LANE, (half + 1) * LANE), slice(cb * LANE, (cb + 1) * LANE))
            to = (slice(cb * LANE, (cb + 1) * LANE), slice(half * LANE, (half + 1) * LANE))
            query32 = query[at].astype(F32)
            plain[to] = (cot[at].astype(F32) * gain[:, at[1]] * query32).T
            gated_q[to] = (query32 * conv[at].astype(F32) * query32).T


def token_scales(total_width, near, far):
    totals = near[...] + far[...]
    inv = lax.rsqrt(totals[0:1, :] / total_width + EPS_NORM)
    return inv, inv * inv * (totals[1:2, :] / total_width)


def send_columns(total_width, plain, gated_q, near, far, mix_cols, cols):
    inv, back = token_scales(total_width, near, far)
    cols[:, 32:64, :] = mix_cols[...]
    for half in range(plain.shape[1] // LANE):
        lo = slice(half * LANE, (half + 1) * LANE)
        for d in range(cols.shape[0]):
            at = (slice(d * 16, d * 16 + 16), lo)
            grad = inv[:, lo] * (plain[at] - back[:, lo] * gated_q[at])
            cols[d, half * 16 : half * 16 + 16, :] = grad.astype(BF16)


def token_grads(total_width, query, conv, cot, gain, near, far, grad_query, gain_part):
    rows = query.shape[0]
    inv_row, back_row = token_scales(total_width, near, far)
    both = jnp.concatenate([inv_row, back_row, jnp.zeros((6, rows), F32)], axis=0)
    for half in range(rows // LANE):
        lo = half * LANE
        turned = jnp.concatenate([both[:, lo : lo + LANE]] * (LANE // 8), axis=0).T
        inv = turned[:, 0:1]
        back = turned[:, 1:2]
        for cb in range(query.shape[1] // LANE):
            at = (slice(lo, lo + LANE), slice(cb * LANE, (cb + 1) * LANE))
            conv32 = conv[at].astype(F32)
            cot32 = cot[at].astype(F32)
            gated = query[at].astype(F32) * conv32
            grad = inv * (cot32 * gain[:, at[1]] - gated * back)
            grad_query[at] = (grad * conv32).astype(BF16)
            part = jnp.sum(cot32 * gated * inv, axis=0, keepdims=True)
            if half == 0:
                gain_part[:, at[1]] = part
            else:
                gain_part[:, at[1]] += part


def correlations(
    scale, cols, filt, skip, gain_part, col_prev,
    back, grad_filt, grad_skip, col_moment,
    conv_s, wide_s, hankel, conv_c, wide_c, mix_out, filt_out,
):
    chans = 16
    peers = cols.shape[0]
    n_tiles = 2 * peers
    segments = 2 * STEP
    lead = 8
    lane = iota((chans, LANE), 1)
    rows_kept = iota((32, LANE), 1) < STEP + STEP * iota((32, LANE), 0)

    def residues(ref, n, first):
        if n < 0 or n >= peers:
            return [jnp.zeros((chans, LANE), F32)] * 2
        return [ref[n, first + tile * 16 : first + tile * 16 + 16, :].astype(F32) for tile in range(2)]

    for d in range(peers):
        conv_s[d * 32 : d * 32 + 32, :] = cols[d, 0:32, :].astype(F32)
    for which, (ref, first) in enumerate([(filt, 0), (cols, 32)]):
        for r in range(STEP):
            wide_s[which * STEP + r, 0 : lead * chans, :] = jnp.zeros((lead * chans, LANE), F32)
        now = residues(ref, -1, first)
        now_rolled = now
        for n in range(-1, peers - 1):
            later = residues(ref, n + 1, first)
            later_rolled = [pltpu.roll(x, HALF, axis=1) for x in later]
            at = slice((lead + n) * chans, (lead + n + 1) * chans)
            for tile in range(2):
                low = which * STEP + 2 * tile
                wide_s[low, at, :] = jnp.where(lane < HALF, now[tile], later_rolled[tile])
                wide_s[low + 1, at, :] = jnp.where(lane < HALF, now_rolled[tile], later[tile])
            now, now_rolled = later, later_rolled
    for b in range(4):
        hankel[b, n_tiles * 32 : (n_tiles + 1) * 32, :] = jnp.zeros((32, LANE), BF16)
        for seg in range(segments):
            wide_c[b, seg, 0 : peers - lead, :] = jnp.zeros((peers - lead, LANE), F32)

    def build(c, b):
        conv_c[b] = conv_s[pl.ds(c, n_tiles, stride=chans), :]
        for seg in range(segments):
            wide_c[b, seg, peers - lead : 2 * peers, :] = wide_s[seg, pl.ds(c, peers + lead, stride=chans), :]

        def turned(k):
            if k == n_tiles:
                return jnp.zeros((32, LANE), F32)
            wide = jnp.broadcast_to(conv_c[b, k : k + 1, :], (32, LANE))
            return pltpu.roll(wide, STEP, axis=1, stride=STEP, stride_axis=0)

        now = turned(0)
        for k in range(n_tiles):
            later = turned(k + 1)
            hankel[b, k * 32 : (k + 1) * 32, :] = jnp.where(rows_kept, now, later).astype(BF16)
            now = later
            if k % 16 == 15:
                yield

    def dots(c, b):
        cuts = 4
        total = None
        for q in reversed(range(cuts)):
            rows = peers // cuts * (q + 1)
            skipped = peers - rows
            left, right = [], []
            for n in range(peers // cuts * q, peers // cuts * (q + 1), 4):
                for half in range(2):
                    at = n + 2 * half + 1 + skipped
                    left.append(
                        jnp.concatenate([wide_c[b, seg, at : at + rows, :] for seg in range(segments)], axis=0).astype(BF16)
                    )
                for k in range(2 * n, 2 * n + 8, 2):
                    for t in (k + 1, k):
                        right.append(
                            jnp.concatenate([hankel[b, 32 * t : 32 * t + 32, :], hankel[b, 32 * t + 32 : 32 * t + 64, :]], axis=1)
                        )
            part = jnp.dot(
                jnp.concatenate(left, axis=1), jnp.concatenate(right, axis=0), preferred_element_type=F32
            )
            yield
            pieces = [part[seg * rows : (seg + 1) * rows] for seg in range(segments)]
            if total is None:
                total = pieces
            else:
                blank = jnp.zeros((skipped, 2 * LANE), F32)
                total = [x + jnp.concatenate([blank, y], axis=0) for x, y in zip(total, pieces)]

        inner = iota((peers, LANE), 1) < LANE - 1
        top = jnp.zeros((1, LANE), F32)

        def later_by_one(x):
            first, second = [pltpu.roll(x[:, t * LANE : (t + 1) * LANE], LANE - 1, axis=1) for t in range(2)]
            below = jnp.concatenate([top, first[:-1]], axis=0)
            return jnp.concatenate([jnp.where(inner, first, second), jnp.where(inner, second, below)], axis=1)

        for which, out in enumerate([mix_out, filt_out]):
            sums = total[which * STEP + STEP - 1]
            for r in reversed(range(STEP - 1)):
                sums = total[which * STEP + r] + later_by_one(sums)
            for tile in range(2):
                out[tile, pl.ds(c, peers, stride=chans), :] = sums[:, tile * LANE : (tile + 1) * LANE]

    def together(*steps):
        for _ in itertools.zip_longest(*steps):
            pass

    together(build(0, 0), build(1, 1))

    def four(i, carry):
        c = 4 * i
        together(build(c + 2, 2), build(c + 3, 3), dots(c, 0), dots(c + 1, 1))
        together(build(jnp.minimum(c + 4, chans - 2), 0), build(jnp.minimum(c + 5, chans - 1), 1), dots(c + 2, 2), dots(c + 3, 3))
        return carry

    lax.fori_loop(0, chans // 4, four, 0)

    diagonal = iota((chans, LANE), 0) == iota((chans, LANE), 1)

    def to_lanes(x):
        return jnp.sum(jnp.where(diagonal, x, 0.0), axis=0, keepdims=True)

    skip_col = jnp.sum(
        jnp.where(diagonal, jnp.concatenate([skip[...], jnp.zeros((1, LANE - chans), F32)], axis=1), 0.0),
        axis=1,
        keepdims=True,
    )
    col_sum = jnp.zeros((chans, LANE), F32)
    for d in range(peers):
        at = slice((peers - 1 - d) * chans, (peers - d) * chans)
        lags = []
        for tile in range(2):
            k = 2 * d + tile
            conv = conv_s[k * chans : (k + 1) * chans, :]
            mix = (mix_out[tile, at, :] * scale + skip_col * conv).astype(BF16)
            back[d, tile * 8 : tile * 8 + 8] = mix.reshape(8, 2, LANE)
            grad = filt_out[tile, at, :] * scale
            grad_filt[:, k * LANE : (k + 1) * LANE] = grad
            squares = grad * grad + EPS_MOMENT
            col_sum = col_sum + squares
            lags.append(jnp.sum(squares, axis=0, keepdims=True))
        part = gain_part[:, d // 8 * LANE : (d // 8 + 1) * LANE]
        high = part.astype(BF16).astype(F32)
        extra = jnp.concatenate(lags + [high, part - high, jnp.zeros((12, LANE), F32)], axis=0)
        back[d, 16:18] = extra.astype(BF16).reshape(8, 2, LANE)[0:2]
    grad_skip[...] = to_lanes(filt_out[0, (peers - 1) * chans : peers * chans, 0:1])[:, :chans]
    mean = to_lanes(jnp.sum(col_sum, axis=1, keepdims=True))[:, :chans] / (n_tiles * LANE)
    col_moment[...] = DECAY * col_prev[...] + (1.0 - DECAY) * mean


def finish(group, back, key, value, row_prev, grad_key, grad_value, row_moment, grad_gain):
    for half in range(key.shape[0] // LANE):
        for cb in range(key.shape[1] // LANE):
            at = (slice(half * LANE, (half + 1) * LANE), slice(cb * LANE, (cb + 1) * LANE))
            block = jnp.concatenate(
                [back[cb * 8 + d, half * 8 : half * 8 + 8].reshape(16, LANE).astype(F32) for d in range(8)], axis=0
            ).T
            grad_key[at] = (block * value[at].astype(F32)).astype(BF16)
            grad_value[at] = (block * key[at].astype(F32)).astype(BF16)
    extra = jnp.zeros((4, LANE), F32)
    for d in range(back.shape[0]):
        extra = extra + back[d, 16:18].reshape(4, LANE).astype(F32)
    lags = jnp.concatenate([extra[0:1], extra[1:2]], axis=1)
    row_moment[...] = DECAY * row_prev[...] + (1.0 - DECAY) * (lags / group)
    gains = jnp.broadcast_to(extra[2:3] + extra[3:4], (8, LANE))
    chans = grad_gain.shape[1]
    place = lax.rem(lax.axis_index("seq"), LANE // chans)
    grad_gain[...] = pltpu.roll(gains, lax.rem(LANE - place * chans, LANE), axis=1)[0:1, :chans]


def sum_over_channels(sums):
    groups = [[4 * x + 2 * z + core for x in range(4) for core in range(2)] for z in range(2)]
    parts = lax.all_to_all(sums, "ch", split_axis=0, concat_axis=0, axis_index_groups=groups, tiled=True)
    here = jnp.sum(parts, axis=0)
    return here, lax.ppermute(here, "ch", [(i, i ^ 2) for i in range(16)])


def correlate_call(chans, span, peers, args):
    return kernel_call(
        functools.partial(correlations, 1.0 / math.sqrt(span)),
        [
            shape((peers, 18, 2, LANE), BF16),
            shape((chans, span), F32),
            shape((1, chans), F32),
            shape((1, chans), F32),
        ],
        args,
        [
            pltpu.VMEM((2 * peers * chans, LANE), F32),
            pltpu.VMEM((2 * STEP, (peers + 8) * chans, LANE), F32),
            pltpu.VMEM((4, (2 * peers + 1) * 32, LANE), BF16),
            pltpu.VMEM((4, 2 * peers, LANE), F32),
            pltpu.VMEM((4, 2 * STEP, 2 * peers, LANE), F32),
            pltpu.VMEM((2, peers * chans, LANE), F32),
            pltpu.VMEM((2, peers * chans, LANE), F32),
        ],
        flops=2 * chans * span * span,
        vmem=40 << 20,
    )


def body(query, key, value, conv, cot, norm_gain, skip_gain, filters, row_prev, col_prev):
    rows, group = query.shape
    n_seq, n_ch = lax.axis_size("seq"), lax.axis_size("ch")
    chans, span = filters.shape[1:]
    (sums,) = kernel_call(
        token_sums,
        [shape((n_ch // 2, 2, rows), F32)],
        [query, conv, cot, norm_gain],
        [pltpu.VMEM((rows, group), BF16)] * 3
        + [pltpu.VMEM((1, group), F32), pltpu.SemaphoreType.DMA((rows // LANE + 1, 3))],
        in_place=(0, 1, 2, 3),
        vmem=60 << 20,
    )
    (mix_cols,) = kernel_call(mix_columns, [shape((n_seq, 32, LANE), BF16)], [key, value])
    (filt_rows,) = kernel_call(filter_rows, [shape((n_seq, 32, LANE), BF16)], [filters[0]])
    near, far = sum_over_channels(sums)
    plain, gated_q = kernel_call(
        turned_products, [shape((group, rows), F32)] * 2, [query, conv, cot, norm_gain]
    )
    (cols,) = kernel_call(
        functools.partial(send_columns, group * n_ch),
        [shape((n_seq, 64, LANE), BF16)],
        [plain, gated_q, near, far, mix_cols],
    )
    grad_query, gain_part = kernel_call(
        functools.partial(token_grads, group * n_ch),
        [shape((rows, group), BF16), shape((1, group), F32)],
        [query, conv, cot, norm_gain, near, far],
    )
    cols = lax.all_to_all(cols, "seq", split_axis=0, concat_axis=0, tiled=True)
    back, grad_filt, grad_skip, col_moment = correlate_call(
        chans, span, n_seq, [cols, filt_rows, skip_gain, gain_part, col_prev]
    )
    back = lax.all_to_all(back, "seq", split_axis=0, concat_axis=0, tiled=True)
    grad_key, grad_value, row_moment, grad_gain = kernel_call(
        functools.partial(finish, group),
        [
            shape((rows, group), BF16),
            shape((rows, group), BF16),
            shape((1, rows), F32),
            shape((1, chans), F32),
        ],
        [back, key, value, row_prev],
    )
    return grad_query, grad_key, grad_value, grad_filt[None], grad_gain, grad_skip, row_moment, col_moment


def solution(mesh):
    tokens = P("seq", "ch")
    owned = P("ch", "seq")
    spread = P("ch", "seq", None)
    return jax.shard_map(
        body,
        mesh=mesh,
        in_specs=(tokens,) * 5 + (P("ch", None), owned, spread, owned, owned),
        out_specs=(tokens,) * 3 + (spread, owned, owned, owned, owned),
        check_vma=False,
    )
```

```python
import functools
import itertools
import math

import jax
import jax.numpy as jnp
from jax import lax
from jax.experimental import pallas as pl
from jax.experimental.pallas import tpu as pltpu
from jax.sharding import PartitionSpec as P

EPS_NORM = 1e-05
EPS_MOMENT = 1e-30
DECAY = 1.0 - 2.0 ** (-0.8)
F32 = jnp.float32
BF16 = jnp.bfloat16
LANE = 128


def iota(shape, axis):
    return lax.broadcasted_iota(jnp.int32, shape, axis)


PITCH = 17
STEP = 4
HALF = 64


def residue_order():
    token, lane = iota((2 * LANE, 2 * LANE), 0), iota((2 * LANE, 2 * LANE), 1)
    source = STEP * (HALF - 1 - lane % HALF) + lane // HALF
    return jnp.where(token == source, 1.0, 0.0).astype(BF16)


def kernel_call(body, outs, args, scratch=(), flops=0, in_place=(), vmem=16 << 20):
    total = sum(math.prod(a.shape) * a.dtype.itemsize for a in list(args) + list(outs))
    return pl.pallas_call(
        body,
        out_shape=tuple(outs),
        in_specs=[pl.BlockSpec(memory_space=pl.ANY if i in in_place else pltpu.VMEM) for i in range(len(args))],
        out_specs=tuple(pl.BlockSpec(memory_space=pltpu.VMEM) for _ in outs),
        scratch_shapes=list(scratch),
        compiler_params=pltpu.CompilerParams(vmem_limit_bytes=vmem),
        cost_estimate=pl.CostEstimate(flops=flops, bytes_accessed=total, transcendentals=0),
    )(*args)


def shape(dims, dtype):
    return jax.ShapeDtypeStruct(dims, dtype)


def token_sums(query_at, conv_at, cot_at, gain_at, out, query, conv, cot, gain, sems):
    rows, width = query.shape
    pairs = [(query_at, query), (conv_at, conv), (cot_at, cot)]
    copies = []
    gain_copy = pltpu.make_async_copy(gain_at, gain, sems.at[rows // LANE, 0])
    gain_copy.start()
    for r in range(rows // LANE):
        at = pl.ds(r * LANE, LANE)
        copies.append([pltpu.make_async_copy(x.at[at], y.at[at], sems.at[r, i]) for i, (x, y) in enumerate(pairs)])
        for copy in copies[-1]:
            copy.start()
    gain_copy.wait()
    gain_row = gain[...]
    for r in range(rows // LANE):
        for copy in copies[r]:
            copy.wait()
        at = slice(r * LANE, (r + 1) * LANE)
        square = jnp.zeros((LANE, LANE), F32)
        dot = jnp.zeros((LANE, LANE), F32)
        for k in range(0, width, LANE):
            gated = query[at, k : k + LANE].astype(F32) * conv[at, k : k + LANE].astype(F32)
            square = square + gated * gated
            dot = dot + cot[at, k : k + LANE].astype(F32) * gain_row[:, k : k + LANE] * gated
        both = jnp.concatenate([jnp.sum(x.T, axis=0, keepdims=True) for x in (square, dot)], axis=0)
        for peer in range(out.shape[0]):
            out[peer, :, at] = both


def mix_columns(key, value, out):
    mixed = (key[...].astype(F32) * value[...].astype(F32)).astype(BF16).astype(F32)
    order = residue_order()
    for cb in range(mixed.shape[1] // LANE):
        block = mixed[:, cb * LANE : (cb + 1) * LANE].T.astype(BF16)
        block = jnp.dot(block, order, preferred_element_type=F32).astype(BF16)
        for d in range(8):
            for tile in range(2):
                out[cb * 8 + d, tile * 16 : tile * 16 + 16, :] = block[
                    d * 16 : d * 16 + 16, tile * LANE : (tile + 1) * LANE
                ]


def filter_rows(filt, out):
    order = residue_order()
    for n in range(filt.shape[1] // (2 * LANE)):
        block = filt[:, n * 2 * LANE : (n + 1) * 2 * LANE].astype(BF16)
        block = jnp.dot(block, order, preferred_element_type=F32).astype(BF16)
        for tile in range(2):
            out[n, tile * 16 : tile * 16 + 16, :] = block[:, tile * LANE : (tile + 1) * LANE]


def turned_products(query, conv, cot, gain, plain, gated_q):
    for half in range(query.shape[0] // LANE):
        for cb in range(query.shape[1] // LANE):
            at = (slice(half * LANE, (half + 1) * LANE), slice(cb * LANE, (cb + 1) * LANE))
            to = (slice(cb * LANE, (cb + 1) * LANE), slice(half * LANE, (half + 1) * LANE))
            query32 = query[at].astype(F32)
            plain[to] = (cot[at].astype(F32) * gain[:, at[1]] * query32).T
            gated_q[to] = (query32 * conv[at].astype(F32) * query32).T


def token_scales(total_width, near, far):
    totals = near[...] + far[...]
    inv = lax.rsqrt(totals[0:1, :] / total_width + EPS_NORM)
    return inv, inv * inv * (totals[1:2, :] / total_width)


def send_columns(total_width, plain, gated_q, near, far, mix_cols, cols):
    inv, back = token_scales(total_width, near, far)
    cols[:, 32:64, :] = mix_cols[...]
    for half in range(plain.shape[1] // LANE):
        lo = slice(half * LANE, (half + 1) * LANE)
        for d in range(cols.shape[0]):
            at = (slice(d * 16, d * 16 + 16), lo)
            grad = inv[:, lo] * (plain[at] - back[:, lo] * gated_q[at])
            cols[d, half * 16 : half * 16 + 16, :] = grad.astype(BF16)


def token_grads(total_width, query, conv, cot, gain, near, far, grad_query, gain_part):
    rows = query.shape[0]
    inv_row, back_row = token_scales(total_width, near, far)
    both = jnp.concatenate([inv_row, back_row, jnp.zeros((6, rows), F32)], axis=0)
    for half in range(rows // LANE):
        lo = half * LANE
        turned = jnp.concatenate([both[:, lo : lo + LANE]] * (LANE // 8), axis=0).T
        inv = turned[:, 0:1]
        back = turned[:, 1:2]
        for cb in range(query.shape[1] // LANE):
            at = (slice(lo, lo + LANE), slice(cb * LANE, (cb + 1) * LANE))
            conv32 = conv[at].astype(F32)
            cot32 = cot[at].astype(F32)
            gated = query[at].astype(F32) * conv32
            grad = inv * (cot32 * gain[:, at[1]] - gated * back)
            grad_query[at] = (grad * conv32).astype(BF16)
            part = jnp.sum(cot32 * gated * inv, axis=0, keepdims=True)
            if half == 0:
                gain_part[:, at[1]] = part
            else:
                gain_part[:, at[1]] += part


def correlations(
    scale, cols, filt, skip, gain_part, col_prev,
    back, grad_filt, grad_skip, col_moment,
    conv_s, wide_s, hankel, conv_c, wide_c, mix_out, filt_out,
):
    chans = 16
    peers = cols.shape[0]
    n_tiles = 2 * peers
    segments = 2 * STEP
    lead = 8
    lane = iota((chans, LANE), 1)
    rows_kept = iota((32, LANE), 1) < STEP + STEP * iota((32, LANE), 0)

    def residues(ref, n, first):
        if n < 0 or n >= peers:
            return [jnp.zeros((chans, LANE), F32)] * 2
        return [ref[n, first + tile * 16 : first + tile * 16 + 16, :].astype(F32) for tile in range(2)]

    for d in range(peers):
        for tile in range(2):
            at = PITCH * (2 * d + tile)
            conv_s[at : at + chans, :] = cols[d, tile * 16 : tile * 16 + 16, :].astype(F32)
    for which, (ref, first) in enumerate([(filt, 0), (cols, 32)]):
        for r in range(STEP):
            wide_s[which * STEP + r, 0 : lead * PITCH, :] = jnp.zeros((lead * PITCH, LANE), F32)
        now = residues(ref, -1, first)
        now_rolled = now
        for n in range(-1, peers - 1):
            later = residues(ref, n + 1, first)
            later_rolled = [pltpu.roll(x, HALF, axis=1) for x in later]
            at = slice((lead + n) * PITCH, (lead + n) * PITCH + chans)
            for tile in range(2):
                low = which * STEP + 2 * tile
                wide_s[low, at, :] = jnp.where(lane < HALF, now[tile], later_rolled[tile])
                wide_s[low + 1, at, :] = jnp.where(lane < HALF, now_rolled[tile], later[tile])
            now, now_rolled = later, later_rolled
    for b in range(4):
        hankel[b, n_tiles * 32 : (n_tiles + 1) * 32, :] = jnp.zeros((32, LANE), BF16)
        for seg in range(segments):
            wide_c[b, seg, 0 : peers - lead, :] = jnp.zeros((peers - lead, LANE), F32)

    def build(c, b):
        conv_c[b] = conv_s[pl.ds(c, n_tiles, stride=PITCH), :]
        for seg in range(segments):
            wide_c[b, seg, peers - lead : 2 * peers, :] = wide_s[seg, pl.ds(c, peers + lead, stride=PITCH), :]

        def turned(k):
            if k == n_tiles:
                return jnp.zeros((32, LANE), F32)
            wide = jnp.broadcast_to(conv_c[b, k : k + 1, :], (32, LANE))
            return pltpu.roll(wide, STEP, axis=1, stride=STEP, stride_axis=0)

        now = turned(0)
        for k in range(n_tiles):
            later = turned(k + 1)
            hankel[b, k * 32 : (k + 1) * 32, :] = jnp.where(rows_kept, now, later).astype(BF16)
            now = later
            if k % 16 == 15:
                yield

    def dots(c, b):
        cuts = 4
        total = None
        for q in reversed(range(cuts)):
            rows = peers // cuts * (q + 1)
            skipped = peers - rows
            left, right = [], []
            for n in range(peers // cuts * q, peers // cuts * (q + 1), 4):
                for half in range(2):
                    at = n + 2 * half + 1 + skipped
                    left.append(
                        jnp.concatenate([wide_c[b, seg, at : at + rows, :] for seg in range(segments)], axis=0).astype(BF16)
                    )
                for k in range(2 * n, 2 * n + 8, 2):
                    for t in (k + 1, k):
                        right.append(
                            jnp.concatenate([hankel[b, 32 * t : 32 * t + 32, :], hankel[b, 32 * t + 32 : 32 * t + 64, :]], axis=1)
                        )
            part = jnp.dot(
                jnp.concatenate(left, axis=1), jnp.concatenate(right, axis=0), preferred_element_type=F32
            )
            yield
            pieces = [part[seg * rows : (seg + 1) * rows] for seg in range(segments)]
            if total is None:
                total = pieces
            else:
                total = [
                    jnp.concatenate([x[:skipped], x[skipped:] + y], axis=0) for x, y in zip(total, pieces)
                ]

        inner = iota((peers, LANE), 1) < LANE - 1
        top = jnp.zeros((1, LANE), F32)

        def later_by_one(x):
            first, second = [pltpu.roll(x[:, t * LANE : (t + 1) * LANE], LANE - 1, axis=1) for t in range(2)]
            below = jnp.concatenate([top, first[:-1]], axis=0)
            return jnp.concatenate([jnp.where(inner, first, second), jnp.where(inner, second, below)], axis=1)

        for which, out in enumerate([mix_out, filt_out]):
            sums = total[which * STEP + STEP - 1]
            for r in reversed(range(STEP - 1)):
                sums = total[which * STEP + r] + later_by_one(sums)
            for tile in range(2):
                out[tile, pl.ds(c, peers, stride=PITCH), :] = sums[:, tile * LANE : (tile + 1) * LANE]

    def together(*steps):
        for _ in itertools.zip_longest(*steps):
            pass

    together(build(0, 0), build(1, 1))

    def four(i, carry):
        c = 4 * i
        together(build(c + 2, 2), build(c + 3, 3), dots(c, 0), dots(c + 1, 1))
        together(build(jnp.minimum(c + 4, chans - 2), 0), build(jnp.minimum(c + 5, chans - 1), 1), dots(c + 2, 2), dots(c + 3, 3))
        return carry

    lax.fori_loop(0, chans // 4, four, 0)

    diagonal = iota((chans, LANE), 0) == iota((chans, LANE), 1)

    def to_lanes(x):
        return jnp.sum(jnp.where(diagonal, x, 0.0), axis=0, keepdims=True)

    skip_col = jnp.sum(
        jnp.where(diagonal, jnp.concatenate([skip[...], jnp.zeros((1, LANE - chans), F32)], axis=1), 0.0),
        axis=1,
        keepdims=True,
    )
    col_sum = jnp.zeros((chans, LANE), F32)
    for d in range(peers):
        at = slice((peers - 1 - d) * PITCH, (peers - 1 - d) * PITCH + chans)
        lags = []
        for tile in range(2):
            k = 2 * d + tile
            conv = conv_s[PITCH * k : PITCH * k + chans, :]
            mix = (mix_out[tile, at, :] * scale + skip_col * conv).astype(BF16)
            back[d, tile * 8 : tile * 8 + 8] = mix.reshape(8, 2, LANE)
            grad = filt_out[tile, at, :] * scale
            grad_filt[:, k * LANE : (k + 1) * LANE] = grad
            squares = grad * grad + EPS_MOMENT
            col_sum = col_sum + squares
            lags.append(jnp.sum(squares, axis=0, keepdims=True))
        part = gain_part[:, d // 8 * LANE : (d // 8 + 1) * LANE]
        high = part.astype(BF16).astype(F32)
        extra = jnp.concatenate(lags + [high, part - high, jnp.zeros((12, LANE), F32)], axis=0)
        back[d, 16:18] = extra.astype(BF16).reshape(8, 2, LANE)[0:2]
    grad_skip[...] = to_lanes(filt_out[0, (peers - 1) * PITCH : (peers - 1) * PITCH + chans, 0:1])[:, :chans]
    mean = to_lanes(jnp.sum(col_sum, axis=1, keepdims=True))[:, :chans] / (n_tiles * LANE)
    col_moment[...] = DECAY * col_prev[...] + (1.0 - DECAY) * mean


def finish(group, back, key, value, row_prev, grad_key, grad_value, row_moment, grad_gain):
    for half in range(key.shape[0] // LANE):
        for cb in range(key.shape[1] // LANE):
            at = (slice(half * LANE, (half + 1) * LANE), slice(cb * LANE, (cb + 1) * LANE))
            block = jnp.concatenate(
                [back[cb * 8 + d, half * 8 : half * 8 + 8].reshape(16, LANE).astype(F32) for d in range(8)], axis=0
            ).T
            grad_key[at] = (block * value[at].astype(F32)).astype(BF16)
            grad_value[at] = (block * key[at].astype(F32)).astype(BF16)
    extra = jnp.zeros((4, LANE), F32)
    for d in range(back.shape[0]):
        extra = extra + back[d, 16:18].reshape(4, LANE).astype(F32)
    lags = jnp.concatenate([extra[0:1], extra[1:2]], axis=1)
    row_moment[...] = DECAY * row_prev[...] + (1.0 - DECAY) * (lags / group)
    gains = jnp.broadcast_to(extra[2:3] + extra[3:4], (8, LANE))
    chans = grad_gain.shape[1]
    place = lax.rem(lax.axis_index("seq"), LANE // chans)
    grad_gain[...] = pltpu.roll(gains, lax.rem(LANE - place * chans, LANE), axis=1)[0:1, :chans]


def sum_over_channels(sums):
    groups = [[4 * x + 2 * z + core for x in range(4) for core in range(2)] for z in range(2)]
    parts = lax.all_to_all(sums, "ch", split_axis=0, concat_axis=0, axis_index_groups=groups, tiled=True)
    here = jnp.sum(parts, axis=0)
    return here, lax.ppermute(here, "ch", [(i, i ^ 2) for i in range(16)])


def correlate_call(chans, span, peers, args):
    return kernel_call(
        functools.partial(correlations, 1.0 / math.sqrt(span)),
        [
            shape((peers, 18, 2, LANE), BF16),
            shape((chans, span), F32),
            shape((1, chans), F32),
            shape((1, chans), F32),
        ],
        args,
        [
            pltpu.VMEM((2 * peers * PITCH, LANE), F32),
            pltpu.VMEM((2 * STEP, (peers + 8) * PITCH, LANE), F32),
            pltpu.VMEM((4, (2 * peers + 1) * 32, LANE), BF16),
            pltpu.VMEM((4, 2 * peers, LANE), F32),
            pltpu.VMEM((4, 2 * STEP, 2 * peers, LANE), F32),
            pltpu.VMEM((2, peers * PITCH, LANE), F32),
            pltpu.VMEM((2, peers * PITCH, LANE), F32),
        ],
        flops=2 * chans * span * span,
        vmem=40 << 20,
    )


def body(query, key, value, conv, cot, norm_gain, skip_gain, filters, row_prev, col_prev):
    rows, group = query.shape
    n_seq, n_ch = lax.axis_size("seq"), lax.axis_size("ch")
    chans, span = filters.shape[1:]
    (sums,) = kernel_call(
        token_sums,
        [shape((n_ch // 2, 2, rows), F32)],
        [query, conv, cot, norm_gain],
        [pltpu.VMEM((rows, group), BF16)] * 3
        + [pltpu.VMEM((1, group), F32), pltpu.SemaphoreType.DMA((rows // LANE + 1, 3))],
        in_place=(0, 1, 2, 3),
        vmem=60 << 20,
    )
    (mix_cols,) = kernel_call(mix_columns, [shape((n_seq, 32, LANE), BF16)], [key, value])
    (filt_rows,) = kernel_call(filter_rows, [shape((n_seq, 32, LANE), BF16)], [filters[0]])
    near, far = sum_over_channels(sums)
    plain, gated_q = kernel_call(
        turned_products, [shape((group, rows), F32)] * 2, [query, conv, cot, norm_gain]
    )
    (cols,) = kernel_call(
        functools.partial(send_columns, group * n_ch),
        [shape((n_seq, 64, LANE), BF16)],
        [plain, gated_q, near, far, mix_cols],
    )
    grad_query, gain_part = kernel_call(
        functools.partial(token_grads, group * n_ch),
        [shape((rows, group), BF16), shape((1, group), F32)],
        [query, conv, cot, norm_gain, near, far],
    )
    cols = lax.all_to_all(cols, "seq", split_axis=0, concat_axis=0, tiled=True)
    back, grad_filt, grad_skip, col_moment = correlate_call(
        chans, span, n_seq, [cols, filt_rows, skip_gain, gain_part, col_prev]
    )
    back = lax.all_to_all(back, "seq", split_axis=0, concat_axis=0, tiled=True)
    grad_key, grad_value, row_moment, grad_gain = kernel_call(
        functools.partial(finish, group),
        [
            shape((rows, group), BF16),
            shape((rows, group), BF16),
            shape((1, rows), F32),
            shape((1, chans), F32),
        ],
        [back, key, value, row_prev],
    )
    return grad_query, grad_key, grad_value, grad_filt[None], grad_gain, grad_skip, row_moment, col_moment


def solution(mesh):
    tokens = P("seq", "ch")
    owned = P("ch", "seq")
    spread = P("ch", "seq", None)
    return jax.shard_map(
        body,
        mesh=mesh,
        in_specs=(tokens,) * 5 + (P("ch", None), owned, spread, owned, owned),
        out_specs=(tokens,) * 3 + (spread, owned, owned, owned, owned),
        check_vma=False,
    )
```

```python
import functools
import itertools
import math

import jax
import jax.numpy as jnp
from jax import lax
from jax.experimental import pallas as pl
from jax.experimental.pallas import tpu as pltpu
from jax.sharding import PartitionSpec as P

EPS_NORM = 1e-05
EPS_MOMENT = 1e-30
DECAY = 1.0 - 2.0 ** (-0.8)
F32 = jnp.float32
BF16 = jnp.bfloat16
LANE = 128


def iota(shape, axis):
    return lax.broadcasted_iota(jnp.int32, shape, axis)


PITCH = 17
STEP = 4
HALF = 64


def residue_order():
    token, lane = iota((2 * LANE, 2 * LANE), 0), iota((2 * LANE, 2 * LANE), 1)
    source = STEP * (HALF - 1 - lane % HALF) + lane // HALF
    return jnp.where(token == source, 1.0, 0.0).astype(BF16)


def kernel_call(body, outs, args, scratch=(), flops=0, in_place=(), vmem=16 << 20):
    total = sum(math.prod(a.shape) * a.dtype.itemsize for a in list(args) + list(outs))
    return pl.pallas_call(
        body,
        out_shape=tuple(outs),
        in_specs=[pl.BlockSpec(memory_space=pl.ANY if i in in_place else pltpu.VMEM) for i in range(len(args))],
        out_specs=tuple(pl.BlockSpec(memory_space=pltpu.VMEM) for _ in outs),
        scratch_shapes=list(scratch),
        compiler_params=pltpu.CompilerParams(vmem_limit_bytes=vmem),
        cost_estimate=pl.CostEstimate(flops=flops, bytes_accessed=total, transcendentals=0),
    )(*args)


def shape(dims, dtype):
    return jax.ShapeDtypeStruct(dims, dtype)


def token_sums(query_at, conv_at, cot_at, gain_at, out, query, conv, cot, gain, sems):
    rows, width = query.shape
    pairs = [(query_at, query), (conv_at, conv), (cot_at, cot)]
    copies = []
    gain_copy = pltpu.make_async_copy(gain_at, gain, sems.at[rows // LANE, 0])
    gain_copy.start()
    for r in range(rows // LANE):
        at = pl.ds(r * LANE, LANE)
        copies.append([pltpu.make_async_copy(x.at[at], y.at[at], sems.at[r, i]) for i, (x, y) in enumerate(pairs)])
        for copy in copies[-1]:
            copy.start()
    gain_copy.wait()
    gain_row = gain[...]
    for r in range(rows // LANE):
        for copy in copies[r]:
            copy.wait()
        at = slice(r * LANE, (r + 1) * LANE)
        square = jnp.zeros((LANE, LANE), F32)
        dot = jnp.zeros((LANE, LANE), F32)
        for k in range(0, width, LANE):
            gated = query[at, k : k + LANE].astype(F32) * conv[at, k : k + LANE].astype(F32)
            square = square + gated * gated
            dot = dot + cot[at, k : k + LANE].astype(F32) * gain_row[:, k : k + LANE] * gated
        both = jnp.concatenate([jnp.sum(x.T, axis=0, keepdims=True) for x in (square, dot)], axis=0)
        for peer in range(out.shape[0]):
            out[peer, :, at] = both


def mix_columns(key, value, out):
    mixed = (key[...].astype(F32) * value[...].astype(F32)).astype(BF16).astype(F32)
    order = residue_order()
    for cb in range(mixed.shape[1] // LANE):
        block = mixed[:, cb * LANE : (cb + 1) * LANE].T.astype(BF16)
        block = jnp.dot(block, order, preferred_element_type=F32).astype(BF16)
        for d in range(8):
            for tile in range(2):
                out[cb * 8 + d, tile * 16 : tile * 16 + 16, :] = block[
                    d * 16 : d * 16 + 16, tile * LANE : (tile + 1) * LANE
                ]


def filter_rows(filt, out):
    order = residue_order()
    for n in range(filt.shape[1] // (2 * LANE)):
        block = filt[:, n * 2 * LANE : (n + 1) * 2 * LANE].astype(BF16)
        block = jnp.dot(block, order, preferred_element_type=F32).astype(BF16)
        for tile in range(2):
            out[n, tile * 16 : tile * 16 + 16, :] = block[:, tile * LANE : (tile + 1) * LANE]


def turned_products(query, conv, cot, gain, plain, gated_q):
    for half in range(query.shape[0] // LANE):
        for cb in range(query.shape[1] // LANE):
            at = (slice(half * LANE, (half + 1) * LANE), slice(cb * LANE, (cb + 1) * LANE))
            to = (slice(cb * LANE, (cb + 1) * LANE), slice(half * LANE, (half + 1) * LANE))
            query32 = query[at].astype(F32)
            plain[to] = (cot[at].astype(F32) * gain[:, at[1]] * query32).T
            gated_q[to] = (query32 * conv[at].astype(F32) * query32).T


def token_scales(total_width, near, far):
    totals = near[...] + far[...]
    inv = lax.rsqrt(totals[0:1, :] / total_width + EPS_NORM)
    return inv, inv * inv * (totals[1:2, :] / total_width)


def send_columns(total_width, plain, gated_q, near, far, mix_cols, cols):
    inv, back = token_scales(total_width, near, far)
    cols[:, 32:64, :] = mix_cols[...]
    for half in range(plain.shape[1] // LANE):
        lo = slice(half * LANE, (half + 1) * LANE)
        for d in range(cols.shape[0]):
            at = (slice(d * 16, d * 16 + 16), lo)
            grad = inv[:, lo] * (plain[at] - back[:, lo] * gated_q[at])
            cols[d, half * 16 : half * 16 + 16, :] = grad.astype(BF16)


def token_grads(total_width, query, conv, cot, gain, near, far, grad_query, gain_part):
    rows = query.shape[0]
    inv_row, back_row = token_scales(total_width, near, far)
    both = jnp.concatenate([inv_row, back_row, jnp.zeros((6, rows), F32)], axis=0)
    for half in range(rows // LANE):
        lo = half * LANE
        turned = jnp.concatenate([both[:, lo : lo + LANE]] * (LANE // 8), axis=0).T
        inv = turned[:, 0:1]
        back = turned[:, 1:2]
        for cb in range(query.shape[1] // LANE):
            at = (slice(lo, lo + LANE), slice(cb * LANE, (cb + 1) * LANE))
            conv32 = conv[at].astype(F32)
            cot32 = cot[at].astype(F32)
            gated = query[at].astype(F32) * conv32
            grad = inv * (cot32 * gain[:, at[1]] - gated * back)
            grad_query[at] = (grad * conv32).astype(BF16)
            part = jnp.sum(cot32 * gated * inv, axis=0, keepdims=True)
            if half == 0:
                gain_part[:, at[1]] = part
            else:
                gain_part[:, at[1]] += part


def correlations(
    scale, cols, filt, skip, gain_part, col_prev,
    back, grad_filt, grad_skip, col_moment,
    conv_s, wide_s, hankel, conv_c, wide_c, mix_out, filt_out,
):
    chans = 16
    peers = cols.shape[0]
    n_tiles = 2 * peers
    segments = 2 * STEP
    lead = 8
    lane = iota((chans, LANE), 1)
    rows_kept = iota((32, LANE), 1) < STEP + STEP * iota((32, LANE), 0)

    def residues(ref, n, first):
        if n < 0 or n >= peers:
            return [jnp.zeros((chans, LANE), F32)] * 2
        return [ref[n, first + tile * 16 : first + tile * 16 + 16, :].astype(F32) for tile in range(2)]

    for d in range(peers):
        for tile in range(2):
            at = PITCH * (2 * d + tile)
            conv_s[at : at + chans, :] = cols[d, tile * 16 : tile * 16 + 16, :].astype(F32)
    for which, (ref, first) in enumerate([(filt, 0), (cols, 32)]):
        for r in range(STEP):
            wide_s[which * STEP + r, 0 : lead * PITCH, :] = jnp.zeros((lead * PITCH, LANE), F32)
        now = residues(ref, -1, first)
        now_rolled = now
        for n in range(-1, peers - 1):
            later = residues(ref, n + 1, first)
            later_rolled = [pltpu.roll(x, HALF, axis=1) for x in later]
            at = slice((lead + n) * PITCH, (lead + n) * PITCH + chans)
            for tile in range(2):
                low = which * STEP + 2 * tile
                wide_s[low, at, :] = jnp.where(lane < HALF, now[tile], later_rolled[tile])
                wide_s[low + 1, at, :] = jnp.where(lane < HALF, now_rolled[tile], later[tile])
            now, now_rolled = later, later_rolled
    for b in range(4):
        hankel[b, n_tiles * 32 : (n_tiles + 1) * 32, :] = jnp.zeros((32, LANE), BF16)
        for seg in range(segments):
            wide_c[b, seg, 0 : peers - lead, :] = jnp.zeros((peers - lead, LANE), F32)

    def build(c, b):
        conv_c[b] = conv_s[pl.ds(c, n_tiles, stride=PITCH), :]
        for seg in range(segments):
            wide_c[b, seg, peers - lead : 2 * peers, :] = wide_s[seg, pl.ds(c, peers + lead, stride=PITCH), :]

        def turned(k):
            if k == n_tiles:
                return jnp.zeros((32, LANE), F32)
            wide = jnp.broadcast_to(conv_c[b, k : k + 1, :], (32, LANE))
            return pltpu.roll(wide, STEP, axis=1, stride=STEP, stride_axis=0)

        now = turned(0)
        for k in range(n_tiles):
            later = turned(k + 1)
            hankel[b, k * 32 : (k + 1) * 32, :] = jnp.where(rows_kept, now, later).astype(BF16)
            now = later
            if k % 16 == 15:
                yield

    def dots(c, b):
        cuts = 4
        total = None
        for q in reversed(range(cuts)):
            rows = peers // cuts * (q + 1)
            skipped = peers - rows
            left, right = [], []
            for n in range(peers // cuts * q, peers // cuts * (q + 1), 4):
                for half in range(2):
                    at = n + 2 * half + 1 + skipped
                    left.append(
                        jnp.concatenate([wide_c[b, seg, at : at + rows, :] for seg in range(segments)], axis=0).astype(BF16)
                    )
                for k in range(2 * n, 2 * n + 8, 2):
                    for t in (k + 1, k):
                        right.append(
                            jnp.concatenate([hankel[b, 32 * t : 32 * t + 32, :], hankel[b, 32 * t + 32 : 32 * t + 64, :]], axis=1)
                        )
            part = jnp.dot(
                jnp.concatenate(left, axis=1), jnp.concatenate(right, axis=0), preferred_element_type=F32
            )
            yield
            pieces = [part[seg * rows : (seg + 1) * rows] for seg in range(segments)]
            if total is None:
                total = pieces
            else:
                total = [
                    jnp.concatenate([x[:skipped], x[skipped:] + y], axis=0) for x, y in zip(total, pieces)
                ]

        inner = iota((peers, LANE), 1) < LANE - 1
        top = jnp.zeros((1, LANE), F32)

        def later_by_one(x):
            first, second = [pltpu.roll(x[:, t * LANE : (t + 1) * LANE], LANE - 1, axis=1) for t in range(2)]
            below = jnp.concatenate([top, first[:-1]], axis=0)
            return jnp.concatenate([jnp.where(inner, first, second), jnp.where(inner, second, below)], axis=1)

        for which, out in enumerate([mix_out, filt_out]):
            sums = total[which * STEP + STEP - 1]
            for r in reversed(range(STEP - 1)):
                sums = total[which * STEP + r] + later_by_one(sums)
            for tile in range(2):
                out[tile, pl.ds(c, peers, stride=PITCH), :] = sums[:, tile * LANE : (tile + 1) * LANE]

    def together(*steps):
        for _ in itertools.zip_longest(*steps):
            pass

    together(build(0, 0), build(1, 1))

    def four(i, carry):
        c = 4 * i
        together(build(c + 2, 2), build(c + 3, 3), dots(c, 0), dots(c + 1, 1))
        together(build(jnp.minimum(c + 4, chans - 2), 0), build(jnp.minimum(c + 5, chans - 1), 1), dots(c + 2, 2), dots(c + 3, 3))
        return carry

    lax.fori_loop(0, chans // 4, four, 0)

    diagonal = iota((chans, LANE), 0) == iota((chans, LANE), 1)

    def to_lanes(x):
        return jnp.sum(jnp.where(diagonal, x, 0.0), axis=0, keepdims=True)

    skip_col = jnp.sum(
        jnp.where(diagonal, jnp.concatenate([skip[...], jnp.zeros((1, LANE - chans), F32)], axis=1), 0.0),
        axis=1,
        keepdims=True,
    )
    col_sum = jnp.zeros((chans, LANE), F32)
    for d in range(peers):
        at = slice((peers - 1 - d) * PITCH, (peers - 1 - d) * PITCH + chans)
        lags = []
        for tile in range(2):
            k = 2 * d + tile
            conv = conv_s[PITCH * k : PITCH * k + chans, :]
            mix = (mix_out[tile, at, :] * scale + skip_col * conv).astype(BF16)
            back[d, tile * 8 : tile * 8 + 8] = mix.reshape(8, 2, LANE)
            grad = filt_out[tile, at, :] * scale
            grad_filt[:, k * LANE : (k + 1) * LANE] = grad
            squares = grad * grad + EPS_MOMENT
            col_sum = col_sum + squares
            lags.append(jnp.sum(squares, axis=0, keepdims=True))
        part = gain_part[:, d // 8 * LANE : (d // 8 + 1) * LANE]
        high = part.astype(BF16).astype(F32)
        extra = jnp.concatenate(lags + [high, part - high, jnp.zeros((12, LANE), F32)], axis=0)
        back[d, 16:18] = extra.astype(BF16).reshape(8, 2, LANE)[0:2]
    grad_skip[...] = to_lanes(filt_out[0, (peers - 1) * PITCH : (peers - 1) * PITCH + chans, 0:1])[:, :chans]
    mean = to_lanes(jnp.sum(col_sum, axis=1, keepdims=True))[:, :chans] / (n_tiles * LANE)
    col_moment[...] = DECAY * col_prev[...] + (1.0 - DECAY) * mean


def finish(group, back, key, value, row_prev, grad_key, grad_value, row_moment, grad_gain):
    for half in range(key.shape[0] // LANE):
        for cb in range(key.shape[1] // LANE):
            at = (slice(half * LANE, (half + 1) * LANE), slice(cb * LANE, (cb + 1) * LANE))
            block = jnp.concatenate(
                [back[cb * 8 + d, half * 8 : half * 8 + 8].reshape(16, LANE).astype(F32) for d in range(8)], axis=0
            ).T
            grad_key[at] = (block * value[at].astype(F32)).astype(BF16)
            grad_value[at] = (block * key[at].astype(F32)).astype(BF16)
    extra = jnp.zeros((4, LANE), F32)
    for d in range(back.shape[0]):
        extra = extra + back[d, 16:18].reshape(4, LANE).astype(F32)
    lags = jnp.concatenate([extra[0:1], extra[1:2]], axis=1)
    row_moment[...] = DECAY * row_prev[...] + (1.0 - DECAY) * (lags / group)
    gains = jnp.broadcast_to(extra[2:3] + extra[3:4], (8, LANE))
    chans = grad_gain.shape[1]
    place = lax.rem(lax.axis_index("seq"), LANE // chans)
    grad_gain[...] = pltpu.roll(gains, lax.rem(LANE - place * chans, LANE), axis=1)[0:1, :chans]


def sum_over_channels(sums):
    groups = [[4 * x + 2 * z + core for x in range(4) for core in range(2)] for z in range(2)]
    parts = lax.all_to_all(sums, "ch", split_axis=0, concat_axis=0, axis_index_groups=groups, tiled=True)
    here = jnp.sum(parts, axis=0)
    return here, lax.ppermute(here, "ch", [(i, i ^ 2) for i in range(16)])


def correlate_call(chans, span, peers, args):
    return kernel_call(
        functools.partial(correlations, 1.0 / math.sqrt(span)),
        [
            shape((peers, 18, 2, LANE), BF16),
            shape((chans, span), F32),
            shape((1, chans), F32),
            shape((1, chans), F32),
        ],
        args,
        [
            pltpu.VMEM(((2 * peers + 1) * PITCH, LANE), F32),
            pltpu.VMEM((2 * STEP, (peers + 9) * PITCH, LANE), F32),
            pltpu.VMEM((4, (2 * peers + 1) * 32, LANE), BF16),
            pltpu.VMEM((4, 2 * peers, LANE), F32),
            pltpu.VMEM((4, 2 * STEP, 2 * peers, LANE), F32),
            pltpu.VMEM((2, (peers + 1) * PITCH, LANE), F32),
            pltpu.VMEM((2, (peers + 1) * PITCH, LANE), F32),
        ],
        flops=2 * chans * span * span,
        vmem=40 << 20,
    )


def body(query, key, value, conv, cot, norm_gain, skip_gain, filters, row_prev, col_prev):
    rows, group = query.shape
    n_seq, n_ch = lax.axis_size("seq"), lax.axis_size("ch")
    chans, span = filters.shape[1:]
    (sums,) = kernel_call(
        token_sums,
        [shape((n_ch // 2, 2, rows), F32)],
        [query, conv, cot, norm_gain],
        [pltpu.VMEM((rows, group), BF16)] * 3
        + [pltpu.VMEM((1, group), F32), pltpu.SemaphoreType.DMA((rows // LANE + 1, 3))],
        in_place=(0, 1, 2, 3),
        vmem=60 << 20,
    )
    (mix_cols,) = kernel_call(mix_columns, [shape((n_seq, 32, LANE), BF16)], [key, value])
    (filt_rows,) = kernel_call(filter_rows, [shape((n_seq, 32, LANE), BF16)], [filters[0]])
    near, far = sum_over_channels(sums)
    plain, gated_q = kernel_call(
        turned_products, [shape((group, rows), F32)] * 2, [query, conv, cot, norm_gain]
    )
    (cols,) = kernel_call(
        functools.partial(send_columns, group * n_ch),
        [shape((n_seq, 64, LANE), BF16)],
        [plain, gated_q, near, far, mix_cols],
    )
    grad_query, gain_part = kernel_call(
        functools.partial(token_grads, group * n_ch),
        [shape((rows, group), BF16), shape((1, group), F32)],
        [query, conv, cot, norm_gain, near, far],
    )
    cols = lax.all_to_all(cols, "seq", split_axis=0, concat_axis=0, tiled=True)
    back, grad_filt, grad_skip, col_moment = correlate_call(
        chans, span, n_seq, [cols, filt_rows, skip_gain, gain_part, col_prev]
    )
    back = lax.all_to_all(back, "seq", split_axis=0, concat_axis=0, tiled=True)
    grad_key, grad_value, row_moment, grad_gain = kernel_call(
        functools.partial(finish, group),
        [
            shape((rows, group), BF16),
            shape((rows, group), BF16),
            shape((1, rows), F32),
            shape((1, chans), F32),
        ],
        [back, key, value, row_prev],
    )
    return grad_query, grad_key, grad_value, grad_filt[None], grad_gain, grad_skip, row_moment, col_moment


def solution(mesh):
    tokens = P("seq", "ch")
    owned = P("ch", "seq")
    spread = P("ch", "seq", None)
    return jax.shard_map(
        body,
        mesh=mesh,
        in_specs=(tokens,) * 5 + (P("ch", None), owned, spread, owned, owned),
        out_specs=(tokens,) * 3 + (spread, owned, owned, owned, owned),
        check_vma=False,
    )
```

```python
import functools
import itertools
import math

import jax
import jax.numpy as jnp
from jax import lax
from jax.experimental import pallas as pl
from jax.experimental.pallas import tpu as pltpu
from jax.sharding import PartitionSpec as P

EPS_NORM = 1e-05
EPS_MOMENT = 1e-30
DECAY = 1.0 - 2.0 ** (-0.8)
F32 = jnp.float32
BF16 = jnp.bfloat16
LANE = 128


def iota(shape, axis):
    return lax.broadcasted_iota(jnp.int32, shape, axis)


PITCH = 17
STEP = 4
HALF = 64


def residue_order():
    token, lane = iota((2 * LANE, 2 * LANE), 0), iota((2 * LANE, 2 * LANE), 1)
    source = STEP * (HALF - 1 - lane % HALF) + lane // HALF
    return jnp.where(token == source, 1.0, 0.0).astype(BF16)


def kernel_call(body, outs, args, scratch=(), flops=0, in_place=(), out_place=(), vmem=16 << 20):
    total = sum(math.prod(a.shape) * a.dtype.itemsize for a in list(args) + list(outs))
    return pl.pallas_call(
        body,
        out_shape=tuple(outs),
        in_specs=[pl.BlockSpec(memory_space=pl.ANY if i in in_place else pltpu.VMEM) for i in range(len(args))],
        out_specs=tuple(
            pl.BlockSpec(memory_space=pl.ANY if i in out_place else pltpu.VMEM) for i in range(len(outs))
        ),
        scratch_shapes=list(scratch),
        compiler_params=pltpu.CompilerParams(vmem_limit_bytes=vmem),
        cost_estimate=pl.CostEstimate(flops=flops, bytes_accessed=total, transcendentals=0),
    )(*args)


def shape(dims, dtype):
    return jax.ShapeDtypeStruct(dims, dtype)


def token_sums(query_at, conv_at, cot_at, gain_at, out, query, conv, cot, gain, sems):
    rows, width = query.shape
    pairs = [(query_at, query), (conv_at, conv), (cot_at, cot)]
    copies = []
    gain_copy = pltpu.make_async_copy(gain_at, gain, sems.at[rows // LANE, 0])
    gain_copy.start()
    for r in range(rows // LANE):
        at = pl.ds(r * LANE, LANE)
        copies.append([pltpu.make_async_copy(x.at[at], y.at[at], sems.at[r, i]) for i, (x, y) in enumerate(pairs)])
        for copy in copies[-1]:
            copy.start()
    gain_copy.wait()
    gain_row = gain[...]
    for r in range(rows // LANE):
        for copy in copies[r]:
            copy.wait()
        at = slice(r * LANE, (r + 1) * LANE)
        square = jnp.zeros((LANE, LANE), F32)
        dot = jnp.zeros((LANE, LANE), F32)
        for k in range(0, width, LANE):
            gated = query[at, k : k + LANE].astype(F32) * conv[at, k : k + LANE].astype(F32)
            square = square + gated * gated
            dot = dot + cot[at, k : k + LANE].astype(F32) * gain_row[:, k : k + LANE] * gated
        both = jnp.concatenate([jnp.sum(x.T, axis=0, keepdims=True) for x in (square, dot)], axis=0)
        for peer in range(out.shape[0]):
            out[peer, :, at] = both


def mix_columns(key, value, out):
    mixed = (key[...].astype(F32) * value[...].astype(F32)).astype(BF16).astype(F32)
    order = residue_order()
    for cb in range(mixed.shape[1] // LANE):
        block = mixed[:, cb * LANE : (cb + 1) * LANE].T.astype(BF16)
        block = jnp.dot(block, order, preferred_element_type=F32).astype(BF16)
        for d in range(8):
            for tile in range(2):
                out[cb * 8 + d, tile * 16 : tile * 16 + 16, :] = block[
                    d * 16 : d * 16 + 16, tile * LANE : (tile + 1) * LANE
                ]


def filter_rows(filt, out):
    order = residue_order()
    for n in range(filt.shape[1] // (2 * LANE)):
        block = filt[:, n * 2 * LANE : (n + 1) * 2 * LANE].astype(BF16)
        block = jnp.dot(block, order, preferred_element_type=F32).astype(BF16)
        for tile in range(2):
            out[n, tile * 16 : tile * 16 + 16, :] = block[:, tile * LANE : (tile + 1) * LANE]


def turned_products(query, conv, cot, gain, plain, gated_q):
    for half in range(query.shape[0] // LANE):
        for cb in range(query.shape[1] // LANE):
            at = (slice(half * LANE, (half + 1) * LANE), slice(cb * LANE, (cb + 1) * LANE))
            to = (slice(cb * LANE, (cb + 1) * LANE), slice(half * LANE, (half + 1) * LANE))
            query32 = query[at].astype(F32)
            plain[to] = (cot[at].astype(F32) * gain[:, at[1]] * query32).T
            gated_q[to] = (query32 * conv[at].astype(F32) * query32).T


def token_scales(total_width, near, far):
    totals = near[...] + far[...]
    inv = lax.rsqrt(totals[0:1, :] / total_width + EPS_NORM)
    return inv, inv * inv * (totals[1:2, :] / total_width)


def send_columns(total_width, plain, gated_q, near, far, mix_cols, cols_at, cols, sems):
    peers, chunk = cols.shape[0], 16
    copies = [pltpu.make_async_copy(mix_cols, cols_at.at[:, pl.ds(32, 32), :], sems.at[peers // chunk])]
    copies[0].start()
    inv, back = token_scales(total_width, near, far)
    for first in range(0, peers, chunk):
        for half in range(plain.shape[1] // LANE):
            lo = slice(half * LANE, (half + 1) * LANE)
            for d in range(first, first + chunk):
                at = (slice(d * 16, d * 16 + 16), lo)
                grad = inv[:, lo] * (plain[at] - back[:, lo] * gated_q[at])
                cols[d, half * 16 : half * 16 + 16, :] = grad.astype(BF16)
        mine = pl.ds(first, chunk)
        copies.append(
            pltpu.make_async_copy(cols.at[mine], cols_at.at[mine, pl.ds(0, 32), :], sems.at[first // chunk])
        )
        copies[-1].start()
    for copy in copies:
        copy.wait()


def token_grads(total_width, query, conv, cot, gain, near, far, grad_query, gain_part):
    rows = query.shape[0]
    inv_row, back_row = token_scales(total_width, near, far)
    both = jnp.concatenate([inv_row, back_row, jnp.zeros((6, rows), F32)], axis=0)
    for half in range(rows // LANE):
        lo = half * LANE
        turned = jnp.concatenate([both[:, lo : lo + LANE]] * (LANE // 8), axis=0).T
        inv = turned[:, 0:1]
        back = turned[:, 1:2]
        for cb in range(query.shape[1] // LANE):
            at = (slice(lo, lo + LANE), slice(cb * LANE, (cb + 1) * LANE))
            conv32 = conv[at].astype(F32)
            cot32 = cot[at].astype(F32)
            gated = query[at].astype(F32) * conv32
            grad = inv * (cot32 * gain[:, at[1]] - gated * back)
            grad_query[at] = (grad * conv32).astype(BF16)
            part = jnp.sum(cot32 * gated * inv, axis=0, keepdims=True)
            if half == 0:
                gain_part[:, at[1]] = part
            else:
                gain_part[:, at[1]] += part


def correlations(
    scale, cols, filt, skip, gain_part, col_prev,
    back, grad_filt, grad_skip, col_moment,
    conv_s, wide_s, hankel, conv_c, wide_c, mix_out, filt_out,
):
    chans = 16
    peers = cols.shape[0]
    n_tiles = 2 * peers
    segments = 2 * STEP
    lead = 8
    lane = iota((chans, LANE), 1)
    rows_kept = iota((32, LANE), 1) < STEP + STEP * iota((32, LANE), 0)

    def residues(ref, n, first):
        if n < 0 or n >= peers:
            return [jnp.zeros((chans, LANE), F32)] * 2
        return [ref[n, first + tile * 16 : first + tile * 16 + 16, :].astype(F32) for tile in range(2)]

    for d in range(peers):
        for tile in range(2):
            at = PITCH * (2 * d + tile)
            conv_s[at : at + chans, :] = cols[d, tile * 16 : tile * 16 + 16, :].astype(F32)
    for which, (ref, first) in enumerate([(filt, 0), (cols, 32)]):
        for r in range(STEP):
            wide_s[which * STEP + r, 0 : lead * PITCH, :] = jnp.zeros((lead * PITCH, LANE), F32)
        now = residues(ref, -1, first)
        now_rolled = now
        for n in range(-1, peers - 1):
            later = residues(ref, n + 1, first)
            later_rolled = [pltpu.roll(x, HALF, axis=1) for x in later]
            at = slice((lead + n) * PITCH, (lead + n) * PITCH + chans)
            for tile in range(2):
                low = which * STEP + 2 * tile
                wide_s[low, at, :] = jnp.where(lane < HALF, now[tile], later_rolled[tile])
                wide_s[low + 1, at, :] = jnp.where(lane < HALF, now_rolled[tile], later[tile])
            now, now_rolled = later, later_rolled
    for b in range(4):
        hankel[b, n_tiles * 32 : (n_tiles + 1) * 32, :] = jnp.zeros((32, LANE), BF16)
        for seg in range(segments):
            wide_c[b, seg, 0 : peers - lead, :] = jnp.zeros((peers - lead, LANE), F32)

    def build(c, b):
        conv_c[b] = conv_s[pl.ds(c, n_tiles, stride=PITCH), :]
        for seg in range(segments):
            wide_c[b, seg, peers - lead : 2 * peers, :] = wide_s[seg, pl.ds(c, peers + lead, stride=PITCH), :]

        def turned(k):
            if k == n_tiles:
                return jnp.zeros((32, LANE), F32)
            wide = jnp.broadcast_to(conv_c[b, k : k + 1, :], (32, LANE))
            return pltpu.roll(wide, STEP, axis=1, stride=STEP, stride_axis=0)

        now = turned(0)
        for k in range(n_tiles):
            later = turned(k + 1)
            hankel[b, k * 32 : (k + 1) * 32, :] = jnp.where(rows_kept, now, later).astype(BF16)
            now = later
            if k % 16 == 15:
                yield

    def dots(c, b):
        cuts = 4
        total = None
        for q in reversed(range(cuts)):
            rows = peers // cuts * (q + 1)
            skipped = peers - rows
            left, right = [], []
            for n in range(peers // cuts * q, peers // cuts * (q + 1), 4):
                for half in range(2):
                    at = n + 2 * half + 1 + skipped
                    left.append(
                        jnp.concatenate([wide_c[b, seg, at : at + rows, :] for seg in range(segments)], axis=0).astype(BF16)
                    )
                for k in range(2 * n, 2 * n + 8, 2):
                    for t in (k + 1, k):
                        right.append(
                            jnp.concatenate([hankel[b, 32 * t : 32 * t + 32, :], hankel[b, 32 * t + 32 : 32 * t + 64, :]], axis=1)
                        )
            part = jnp.dot(
                jnp.concatenate(left, axis=1), jnp.concatenate(right, axis=0), preferred_element_type=F32
            )
            yield
            pieces = [part[seg * rows : (seg + 1) * rows] for seg in range(segments)]
            if total is None:
                total = pieces
            else:
                total = [
                    jnp.concatenate([x[:skipped], x[skipped:] + y], axis=0) for x, y in zip(total, pieces)
                ]

        inner = iota((peers, LANE), 1) < LANE - 1
        top = jnp.zeros((1, LANE), F32)

        def later_by_one(x):
            first, second = [pltpu.roll(x[:, t * LANE : (t + 1) * LANE], LANE - 1, axis=1) for t in range(2)]
            below = jnp.concatenate([top, first[:-1]], axis=0)
            return jnp.concatenate([jnp.where(inner, first, second), jnp.where(inner, second, below)], axis=1)

        for which, out in enumerate([mix_out, filt_out]):
            sums = total[which * STEP + STEP - 1]
            for r in reversed(range(STEP - 1)):
                sums = total[which * STEP + r] + later_by_one(sums)
            for tile in range(2):
                out[tile, pl.ds(c, peers, stride=PITCH), :] = sums[:, tile * LANE : (tile + 1) * LANE]

    def together(*steps):
        for _ in itertools.zip_longest(*steps):
            pass

    together(build(0, 0), build(1, 1))

    def four(i, carry):
        c = 4 * i
        together(build(c + 2, 2), build(c + 3, 3), dots(c, 0), dots(c + 1, 1))
        together(build(jnp.minimum(c + 4, chans - 2), 0), build(jnp.minimum(c + 5, chans - 1), 1), dots(c + 2, 2), dots(c + 3, 3))
        return carry

    lax.fori_loop(0, chans // 4, four, 0)

    diagonal = iota((chans, LANE), 0) == iota((chans, LANE), 1)

    def to_lanes(x):
        return jnp.sum(jnp.where(diagonal, x, 0.0), axis=0, keepdims=True)

    skip_col = jnp.sum(
        jnp.where(diagonal, jnp.concatenate([skip[...], jnp.zeros((1, LANE - chans), F32)], axis=1), 0.0),
        axis=1,
        keepdims=True,
    )
    col_sum = jnp.zeros((chans, LANE), F32)
    for d in range(peers):
        at = slice((peers - 1 - d) * PITCH, (peers - 1 - d) * PITCH + chans)
        lags = []
        for tile in range(2):
            k = 2 * d + tile
            conv = conv_s[PITCH * k : PITCH * k + chans, :]
            mix = (mix_out[tile, at, :] * scale + skip_col * conv).astype(BF16)
            back[d, tile * 8 : tile * 8 + 8] = mix.reshape(8, 2, LANE)
            grad = filt_out[tile, at, :] * scale
            grad_filt[:, k * LANE : (k + 1) * LANE] = grad
            squares = grad * grad + EPS_MOMENT
            col_sum = col_sum + squares
            lags.append(jnp.sum(squares, axis=0, keepdims=True))
        part = gain_part[:, d // 8 * LANE : (d // 8 + 1) * LANE]
        high = part.astype(BF16).astype(F32)
        extra = jnp.concatenate(lags + [high, part - high, jnp.zeros((12, LANE), F32)], axis=0)
        back[d, 16:18] = extra.astype(BF16).reshape(8, 2, LANE)[0:2]
    grad_skip[...] = to_lanes(filt_out[0, (peers - 1) * PITCH : (peers - 1) * PITCH + chans, 0:1])[:, :chans]
    mean = to_lanes(jnp.sum(col_sum, axis=1, keepdims=True))[:, :chans] / (n_tiles * LANE)
    col_moment[...] = DECAY * col_prev[...] + (1.0 - DECAY) * mean


def finish(group, back, key, value, row_prev, grad_key, grad_value, row_moment, grad_gain):
    for half in range(key.shape[0] // LANE):
        for cb in range(key.shape[1] // LANE):
            at = (slice(half * LANE, (half + 1) * LANE), slice(cb * LANE, (cb + 1) * LANE))
            block = jnp.concatenate(
                [back[cb * 8 + d, half * 8 : half * 8 + 8].reshape(16, LANE).astype(F32) for d in range(8)], axis=0
            ).T
            grad_key[at] = (block * value[at].astype(F32)).astype(BF16)
            grad_value[at] = (block * key[at].astype(F32)).astype(BF16)
    extra = jnp.zeros((4, LANE), F32)
    for d in range(back.shape[0]):
        extra = extra + back[d, 16:18].reshape(4, LANE).astype(F32)
    lags = jnp.concatenate([extra[0:1], extra[1:2]], axis=1)
    row_moment[...] = DECAY * row_prev[...] + (1.0 - DECAY) * (lags / group)
    gains = jnp.broadcast_to(extra[2:3] + extra[3:4], (8, LANE))
    chans = grad_gain.shape[1]
    place = lax.rem(lax.axis_index("seq"), LANE // chans)
    grad_gain[...] = pltpu.roll(gains, lax.rem(LANE - place * chans, LANE), axis=1)[0:1, :chans]


def sum_over_channels(sums):
    groups = [[4 * x + 2 * z + core for x in range(4) for core in range(2)] for z in range(2)]
    parts = lax.all_to_all(sums, "ch", split_axis=0, concat_axis=0, axis_index_groups=groups, tiled=True)
    here = jnp.sum(parts, axis=0)
    return here, lax.ppermute(here, "ch", [(i, i ^ 2) for i in range(16)])


def correlate_call(chans, span, peers, args):
    return kernel_call(
        functools.partial(correlations, 1.0 / math.sqrt(span)),
        [
            shape((peers, 18, 2, LANE), BF16),
            shape((chans, span), F32),
            shape((1, chans), F32),
            shape((1, chans), F32),
        ],
        args,
        [
            pltpu.VMEM(((2 * peers + 1) * PITCH, LANE), F32),
            pltpu.VMEM((2 * STEP, (peers + 9) * PITCH, LANE), F32),
            pltpu.VMEM((4, (2 * peers + 1) * 32, LANE), BF16),
            pltpu.VMEM((4, 2 * peers, LANE), F32),
            pltpu.VMEM((4, 2 * STEP, 2 * peers, LANE), F32),
            pltpu.VMEM((2, (peers + 1) * PITCH, LANE), F32),
            pltpu.VMEM((2, (peers + 1) * PITCH, LANE), F32),
        ],
        flops=2 * chans * span * span,
        vmem=40 << 20,
    )


def body(query, key, value, conv, cot, norm_gain, skip_gain, filters, row_prev, col_prev):
    rows, group = query.shape
    n_seq, n_ch = lax.axis_size("seq"), lax.axis_size("ch")
    chans, span = filters.shape[1:]
    (sums,) = kernel_call(
        token_sums,
        [shape((n_ch // 2, 2, rows), F32)],
        [query, conv, cot, norm_gain],
        [pltpu.VMEM((rows, group), BF16)] * 3
        + [pltpu.VMEM((1, group), F32), pltpu.SemaphoreType.DMA((rows // LANE + 1, 3))],
        in_place=(0, 1, 2, 3),
        vmem=60 << 20,
    )
    (mix_cols,) = kernel_call(mix_columns, [shape((n_seq, 32, LANE), BF16)], [key, value])
    (filt_rows,) = kernel_call(filter_rows, [shape((n_seq, 32, LANE), BF16)], [filters[0]])
    near, far = sum_over_channels(sums)
    plain, gated_q = kernel_call(
        turned_products, [shape((group, rows), F32)] * 2, [query, conv, cot, norm_gain]
    )
    (cols,) = kernel_call(
        functools.partial(send_columns, group * n_ch),
        [shape((n_seq, 64, LANE), BF16)],
        [plain, gated_q, near, far, mix_cols],
        [pltpu.VMEM((n_seq, 32, LANE), BF16), pltpu.SemaphoreType.DMA((n_seq // 16 + 1,))],
        out_place=(0,),
    )
    grad_query, gain_part = kernel_call(
        functools.partial(token_grads, group * n_ch),
        [shape((rows, group), BF16), shape((1, group), F32)],
        [query, conv, cot, norm_gain, near, far],
    )
    cols = lax.all_to_all(cols, "seq", split_axis=0, concat_axis=0, tiled=True)
    back, grad_filt, grad_skip, col_moment = correlate_call(
        chans, span, n_seq, [cols, filt_rows, skip_gain, gain_part, col_prev]
    )
    back = lax.all_to_all(back, "seq", split_axis=0, concat_axis=0, tiled=True)
    grad_key, grad_value, row_moment, grad_gain = kernel_call(
        functools.partial(finish, group),
        [
            shape((rows, group), BF16),
            shape((rows, group), BF16),
            shape((1, rows), F32),
            shape((1, chans), F32),
        ],
        [back, key, value, row_prev],
    )
    return grad_query, grad_key, grad_value, grad_filt[None], grad_gain, grad_skip, row_moment, col_moment


def solution(mesh):
    tokens = P("seq", "ch")
    owned = P("ch", "seq")
    spread = P("ch", "seq", None)
    return jax.shard_map(
        body,
        mesh=mesh,
        in_specs=(tokens,) * 5 + (P("ch", None), owned, spread, owned, owned),
        out_specs=(tokens,) * 3 + (spread, owned, owned, owned, owned),
        check_vma=False,
    )
```
